32 devices in a mesh: dp: 8 (over z, y), seq: 4 (over x, core).
Axes of the slice: x: 2, y: 2, z: 4, core: 2. Of those that a mesh axis runs over, the one named last changes fastest.
Arguments:
- tokens: bfloat16 [8192, 768], P(('dp', 'seq')), may hold values from -6 to 6
- lengths: int32 [8], P('dp'), may hold values from 769 to 1024, as said below
- cotangent: bfloat16 [8192, 768], P(('dp', 'seq')), may hold values from -6 to 6
- w_gate: bfloat16 [2, 768, 1536], P(None, ('dp', 'seq')), may hold values from -0.21875 to 0.21875
- w_value: bfloat16 [2, 768, 3072], P(None, ('dp', 'seq')), may hold values from -0.21875 to 0.21875
- w_mix: bfloat16 [2, 1536, 1536], P(None, ('dp', 'seq')), may hold values from -0.15625 to 0.15625
- w_out: bfloat16 [2, 1536, 768], P(None, ('dp', 'seq')), may hold values from -0.4375 to 0.4375
- ln_gain: bfloat16 [2, 768], P(None, ('dp', 'seq')), may hold values from 0.5 to 1.5
- ln_bias: bfloat16 [2, 768], P(None, ('dp', 'seq')), may hold values from -1.5 to 1.5
- ssm_coef: float32 [2, 2, 1536, 64], P(None, None, 'seq'), may hold values from -1.5 to 1.5
- ssm_rate: float32 [2, 2, 1536, 64], P(None, None, 'seq'), may hold values from 0.00029296876 to 0.033
- ssm_skip: float32 [2, 2, 1536], P(None, None, 'seq'), may hold values from -4 to 4
Outputs:
- output: float32 [8192, 768], P(('dp', 'seq'))
- grad_tokens: float32 [8192, 768], P(('dp', 'seq'))
- grad_w_gate: float32 [2, 768, 1536], P(None, ('dp', 'seq'))
- grad_w_value: float32 [2, 768, 3072], P(None, ('dp', 'seq'))
- grad_w_mix: float32 [2, 1536, 1536], P(None, ('dp', 'seq'))
- grad_w_out: float32 [2, 1536, 768], P(None, ('dp', 'seq'))
- grad_ln_gain: float32 [2, 768], P(None, ('dp', 'seq'))
- grad_ln_bias: float32 [2, 768], P(None, ('dp', 'seq'))
- grad_ssm_coef: float32 [2, 2, 1536, 64], P(None, None, 'seq')
- grad_ssm_rate: float32 [2, 2, 1536, 64], P(None, None, 'seq')
- grad_ssm_skip: float32 [2, 2, 1536], P(None, None, 'seq')
The draws below stay inside these ranges and needn't reach their ends.
Inputs may be any that keep to these rules, and one draw needn't show every extreme that they name: `lengths`: every sequence ends within the rows of the last device of seq; in each draw at least one slot is full.
All inputs are finite; a program needn't handle non-finite values.
Results may differ from the reference program's by a relative error of at most 0.02.
Values may be sent and summed in bfloat16 or wider, within the bound.
No kernel may reach another device: no remote copies, remote signals or barrier semaphores. Data moves between devices by JAX's collectives and lax.ppermute only.
A program may use at most 448 MiB of HBM per device.

```python
import math
from functools import partial
import jax
import jax.numpy as jnp
from jax import lax

D = 768
SSM = 1536
STATE = 64
LAYERS = 2
VALUE = 3072
SLOT = 1024
ROWS = 256
TOKENS = 8192
N_DP = 8


def draw_lengths(key, part):
    key = jax.random.fold_in(key, 11)
    first_key, second_key = jax.random.split(key)
    shorter = SLOT - jax.random.randint(first_key, (N_DP,), 0, ROWS)
    chosen = jax.random.randint(second_key, (), 0, N_DP)
    return jnp.where(jnp.arange(N_DP) == chosen, SLOT, shorter).astype(jnp.int32)


def shard_levels(own_key, shape, cuts, smallest, top_value):
    factor_of = 1.0
    for dim, shards_of in cuts:
        heights = jax.random.uniform(jax.random.fold_in(jax.random.fold_in(own_key, 6), dim), (shards_of,), jnp.float32, smallest / len(cuts), top_value / len(cuts))
        factor_of = factor_of * jnp.repeat(jnp.exp(heights), shape[dim] // shards_of).reshape((-1,) + (1,) * (len(shape) - 1 - dim))
    return factor_of


def normal_values(own_key, extent, scale, bound, shards=(), kind=jnp.bfloat16):
    array = jax.random.normal(own_key, extent, jnp.float32) * scale
    if len(shards) > 0:
        array = shard_levels(own_key, extent, shards, -0.22, 0.18) * array
    return jnp.clip(array, min=-bound, max=bound).astype(kind)


def setup_inputs(seed: int = 0) -> dict:
    splits = jax.random.split(jax.random.key(seed), 13)
    return {
        "tokens": normal_values(splits[0], (TOKENS, D), 1.0, 6.0, ((0, 32),)),
        "lengths": draw_lengths(jax.random.fold_in(splits[12], 71), 0),
        "cotangent": normal_values(splits[2], (TOKENS, D), 1.0, 6.0, ((0, 32),)),
        "w_gate": normal_values(splits[3], (LAYERS, D, SSM), D ** -0.5, 0.21875, ((1, 32),)),
        "w_value": normal_values(splits[4], (LAYERS, D, VALUE), D ** -0.5, 0.21875, ((1, 32),)),
        "w_mix": normal_values(splits[5], (LAYERS, SSM, SSM), SSM ** -0.5, 0.15625, ((1, 32),)),
        "w_out": normal_values(splits[6], (LAYERS, SSM, D), (SSM // 8) ** -0.5, 0.4375, ((1, 32),)),
        "ln_gain": jnp.clip(1.0 + 0.1 * jax.random.normal(splits[7], (LAYERS, D), jnp.float32), 0.5, 1.5).astype(jnp.bfloat16),
        "ln_bias": normal_values(splits[8], (LAYERS, D), 0.3, 1.5, ((1, 32),)),
        "ssm_coef": normal_values(splits[9], (LAYERS, 2, SSM, STATE), 0.25, 1.5, ((2, 4),), jnp.float32),
        "ssm_rate": jnp.clip(jnp.exp(math.log(0.033) - 4.724197 * jax.random.uniform(splits[10], (LAYERS, 2, SSM, STATE), jnp.float32) ** shard_levels(splits[10], (LAYERS, 2, SSM, STATE), ((2, 4),), -0.2, 0.2)), 0.00029296876, 0.033),
        "ssm_skip": normal_values(splits[11], (LAYERS, 2, SSM), 1.0, 4.0, ((2, 4),), jnp.float32),
    }


EPSILON = 1e-05
PRECISE = lax.Precision.HIGHEST

@jax.custom_vjp
def low(v):
    return lax.optimization_barrier(v.astype(jnp.bfloat16)).astype(jnp.float32)

@jax.custom_vjp
def low_back(v):
    return v

def low_keep(v):
    return (low(v), None)

def low_pass(kept, grad):
    return (grad,)

def back_keep(v):
    return (v, None)

def back_low(kept, grad):
    return (low(grad),)
low.defvjp(low_keep, low_pass)
low_back.defvjp(back_keep, back_low)

def gelu_exact(values):
    return jax.nn.gelu(values, approximate=False)

def kernel_block(offsets, pair):
    coef_rows, rate_rows = pair
    decays = jnp.exp(-rate_rows[:, :, None] * offsets[None, None, :])
    return lax.optimization_barrier(jnp.sum((coef_rows * rate_rows)[:, :, None] * decays, axis=1))

def kernels(ssm_coef, ssm_rate):
    offsets = jnp.arange(SLOT, dtype=jnp.float32)
    row_total = LAYERS * 2 * SSM
    coef_blocks = ssm_coef.reshape(row_total // 64, 64, STATE)
    rate_blocks = ssm_rate.reshape(row_total // 64, 64, STATE)
    result = lax.map(jax.checkpoint(partial(kernel_block, offsets)), (coef_blocks, rate_blocks))
    return result.reshape(LAYERS, 2, SSM, SLOT)

def causal_conv(series, kernel):
    series_len = series.shape[0]
    spectrum = jnp.fft.rfft(series, n=2 * series_len, axis=0) * jnp.fft.rfft(kernel.T, n=2 * series_len, axis=0)
    return jnp.fft.irfft(spectrum, n=2 * series_len, axis=0)[:series_len]

def layer_forward(stream, keep_rows, weights, kernel, skip_pair):
    w_gate, w_value, w_mix, w_out, ln_scale, ln_shift = weights
    centre = lax.optimization_barrier(jnp.mean(stream, axis=-1, keepdims=True))
    centred = stream - centre
    spread = lax.optimization_barrier(jnp.mean(centred * centred, axis=-1, keepdims=True))
    normed = low(centred * lax.rsqrt(spread + EPSILON) * ln_scale + ln_shift)
    gate_pre = low_back(jnp.dot(normed, w_gate, precision=PRECISE))
    value_pre = low_back(jnp.dot(normed, w_value, precision=PRECISE))
    gate_act = gelu_exact(gate_pre)
    values = low(low_back(gelu_exact(value_pre) * keep_rows))
    ahead = values[:, :SSM]
    behind = values[:, SSM:]
    forward_mix = causal_conv(ahead, kernel[0]) + skip_pair[0] * ahead
    backward_mix = jnp.flip(causal_conv(jnp.flip(behind, 0), kernel[1]), 0) + skip_pair[1] * behind
    product = low(low_back(forward_mix * backward_mix))
    update = low_back(jnp.dot(product, w_mix, precision=PRECISE))
    mixed = low(update * gate_act)
    return stream + low_back(jnp.dot(mixed, w_out, precision=PRECISE))

def group_forward(length, stream, w_gate, w_value, w_mix, w_out, ln_gain, ln_bias, kernel, ssm_skip):
    positions = jnp.arange(stream.shape[0], dtype=jnp.int32)
    keep_rows = (positions < length).astype(jnp.float32)[:, None]
    for layer in range(LAYERS):
        weights = (w_gate[layer], w_value[layer], w_mix[layer], w_out[layer], ln_gain[layer], ln_bias[layer])
        stream = layer_forward(stream, keep_rows, weights, kernel[layer], ssm_skip[layer])
    return stream

def reference(tokens, lengths, cotangent, w_gate, w_value, w_mix, w_out, ln_gain, ln_bias, ssm_coef, ssm_rate, ssm_skip):
    inputs = tokens.astype(jnp.float32).reshape(N_DP, SLOT, D)
    targets = cotangent.astype(jnp.float32).reshape(N_DP, SLOT, D)
    params = tuple((param.astype(jnp.float32) for param in (w_gate, w_value, w_mix, w_out, ln_gain, ln_bias)))
    kernel, kernel_pull = jax.vjp(kernels, ssm_coef, ssm_rate)
    params = params + (kernel, ssm_skip)

    def step(totals, item):
        stream, target, length = item
        result, pull = jax.vjp(partial(group_forward, length), stream, *params)
        grads = pull(target)
        totals = tuple((total + extra for total, extra in zip(totals, grads[1:])))
        return (totals, (result, grads[0]))
    zeros = tuple((jnp.zeros_like(param) for param in params))
    totals, (outputs, input_grads) = lax.scan(step, zeros, (inputs, targets, lengths))
    coef_grad, rate_grad = kernel_pull(totals[6])
    return (outputs.reshape(TOKENS, D), input_grads.reshape(TOKENS, D), totals[0], totals[1], totals[2], totals[3], totals[4], totals[5], coef_grad, rate_grad, totals[7])
```

```python
import numpy as np

import jax
import jax.numpy as jnp
from jax import lax
from jax.sharding import PartitionSpec as P

EPSILON = 1e-05
BF = jnp.bfloat16
F32 = jnp.float32
LAG_BLOCK = 128


def dot(left, right, left_dim, right_dim):
    return lax.dot_general(
        left, right, (((left_dim,), (right_dim,)), ((), ())), preferred_element_type=F32
    )


def wave_table(length):
    turns = 4 * length
    step = np.arange(length, dtype=np.int64)
    phase = ((2 * step[:, None] + 1) * step[None, :]) % turns
    angle = phase * (2.0 * np.pi / turns)
    return np.concatenate([np.cos(angle), np.sin(angle)], 0).astype(jnp.bfloat16)


def seq_pairs(count, bit):
    return [(i, i ^ bit) for i in range(count)]


def seq_gather(block, count):
    blocks = {0: block}
    bit = count // 2
    while bit:
        for member in list(blocks):
            blocks[member ^ bit] = lax.ppermute(blocks[member], "seq", seq_pairs(count, bit))
        bit //= 2
    return [blocks[m] for m in range(count)]


def seq_reduce(blocks, count):
    blocks = dict(enumerate(blocks))
    bit = 1
    while bit < count:
        for member in sorted(blocks, reverse=True):
            if member & bit:
                sent = blocks.pop(member).astype(BF)
                came = lax.ppermute(sent, "seq", seq_pairs(count, bit))
                blocks[member ^ bit] = blocks[member ^ bit] + came.astype(F32)
        bit *= 2
    return blocks[0]


def gelu_parts(pre):
    share = 0.5 * (1.0 + lax.erf(pre * np.float32(np.sqrt(0.5))))
    slope = share + pre * (jnp.exp(-0.5 * pre * pre) * np.float32(1.0 / np.sqrt(2.0 * np.pi)))
    return pre * share, slope


def normalize(stream):
    centre = jnp.mean(stream, axis=-1, keepdims=True)
    centred = stream - centre
    spread = jnp.mean(centred * centred, axis=-1, keepdims=True)
    factor = lax.rsqrt(spread + EPSILON)
    return centred * factor, factor


def lag_factors(rates, length):
    block = min(LAG_BLOCK, length)
    far = jnp.exp(-rates[:, None, :] * (block * jnp.arange(length // block, dtype=F32))[None, :, None])
    near = jnp.exp(-rates[:, None, :] * jnp.arange(block, dtype=F32)[None, :, None])
    return far, near


def lag_kernels(coef, rates, length):
    far, near = lag_factors(rates, length)
    left = ((coef * rates)[:, None, :] * far).astype(BF)
    kern = lax.dot_general(
        left, near.astype(BF), (((2,), (2,)), ((0,), (0,))), preferred_element_type=F32
    )
    return kern.reshape(coef.shape[0], length)


def lag_grads(coef, rates, kern_grad, length):
    far, near = lag_factors(rates, length)
    block = near.shape[1]
    lags = jnp.arange(block, dtype=F32)[None, :, None]
    pair = jnp.concatenate([near, near * lags], axis=2).astype(BF)
    pieces = kern_grad.reshape(rates.shape[0], length // block, block).astype(BF)
    sums = lax.dot_general(pieces, pair, (((2,), (1,)), ((0,), (0,))), preferred_element_type=F32)
    states = rates.shape[1]
    plain = sums[:, :, :states]
    starts = (block * jnp.arange(length // block, dtype=F32))[None, :, None]
    total = jnp.sum(far * plain, axis=1)
    moment = jnp.sum(far * (starts * plain + sums[:, :, states:]), axis=1)
    return rates * total, coef * (total - rates * moment)


def spectrum_of(waves, series):
    both = dot(waves, series, 1, 0)
    half = both.shape[0] // 2
    return both[:half], both[half:]


def series_of(waves, cos_part, sin_part):
    half = cos_part.shape[0]
    both = jnp.concatenate([cos_part, sin_part], 0).astype(BF)
    return dot(waves, both, 0, 0) * (1.0 / half)


def run_layer(stream, keep, weights, kernel_hat, skip, waves, count):
    w_gate, w_value, w_mix, w_out, gain, bias = weights
    xhat, factor = normalize(stream)
    normed_own = (xhat * gain + bias).astype(BF)
    normed = jnp.concatenate(seq_gather(normed_own, count), 0)
    gate_act, gate_slope = gelu_parts(dot(normed, w_gate, 1, 0))
    value_act, value_slope = gelu_parts(dot(normed, w_value, 1, 0))
    values = (value_act * keep).astype(BF)
    value_slope = (value_slope * keep).astype(BF)
    x_cos, x_sin = spectrum_of(waves, values)
    k_cos, k_sin = kernel_hat
    mixes = series_of(waves, k_cos * x_cos - k_sin * x_sin, k_cos * x_sin + k_sin * x_cos)
    mixes = mixes + skip * values.astype(F32)
    width = mixes.shape[1] // 2
    product = (mixes[:, :width] * mixes[:, width:]).astype(BF)
    rows = stream.shape[0]
    products = []
    for member, came in enumerate(seq_gather(product, count)):
        pieces = came.reshape(count, rows, width)
        products.append(jnp.concatenate([pieces[m ^ member] for m in range(count)], 0))
    update = dot(products[0], w_mix[0], 1, 0)
    for member in range(1, count):
        update = update + dot(products[member], w_mix[member], 1, 0)
    mixed = (update * gate_act).astype(BF)
    partial = dot(mixed, w_out, 1, 0)
    result = stream + seq_reduce(
        [partial[m * rows : (m + 1) * rows] for m in range(count)], count
    )
    saved = (
        xhat,
        factor,
        normed,
        gate_act.astype(BF),
        (update * gate_slope).astype(BF),
        value_slope,
        values,
        (x_cos.astype(BF), x_sin.astype(BF)),
        mixes.astype(BF),
        products,
        mixed,
    )
    return result, saved


def back_layer(grad_stream, saved, weights, kernel_hat, skip, waves, count):
    w_gate, w_value, w_mix, w_out, gain, bias = weights
    xhat, factor, normed, gate_act, gate_back, value_slope, values, x_hat, mixes, products, mixed = saved
    rows = grad_stream.shape[0]
    out_low = jnp.concatenate(seq_gather(grad_stream.astype(BF), count), 0)
    grad_mixed = dot(out_low, w_out, 1, 1)
    grad_out = dot(mixed, out_low, 0, 0)
    update_low = (grad_mixed * gate_act.astype(F32)).astype(BF)
    gate_grad = (grad_mixed * gate_back.astype(F32)).astype(BF)
    width = products[0].shape[1]
    partials = []
    for member in range(count):
        part = dot(update_low, w_mix[member], 1, 1).reshape(count, rows, width)
        partials.append(jnp.concatenate([part[m ^ member] for m in range(count)], 0))
    product_low = seq_reduce(partials, count).astype(BF).astype(F32)
    grad_mix = [dot(products[member], update_low, 0, 0) for member in range(count)]
    mixes = mixes.astype(F32)
    back = jnp.concatenate([product_low * mixes[:, width:], product_low * mixes[:, :width]], 1)
    back_low = back.astype(BF)
    g_cos, g_sin = spectrum_of(waves, back_low)
    k_cos, k_sin = kernel_hat
    grad_values = series_of(waves, k_cos * g_cos + k_sin * g_sin, k_cos * g_sin - k_sin * g_cos)
    grad_values = grad_values + skip * back
    x_cos, x_sin = x_hat
    x_cos = x_cos.astype(F32)
    x_sin = x_sin.astype(F32)
    kern_hat = (g_cos * x_cos + g_sin * x_sin, g_sin * x_cos - g_cos * x_sin)
    grad_skip = jnp.sum(back * values.astype(F32), axis=0)
    value_grad = (grad_values.astype(BF).astype(F32) * value_slope.astype(F32)).astype(BF)
    grad_value = dot(normed, value_grad, 0, 0)
    grad_gate = dot(normed, gate_grad, 0, 0)
    partial = dot(value_grad, w_value, 1, 1) + dot(gate_grad, w_gate, 1, 1)
    grad_normed = seq_reduce([partial[m * rows : (m + 1) * rows] for m in range(count)], count)
    norm_terms = jnp.stack([jnp.sum(grad_normed * xhat, 0), jnp.sum(grad_normed, 0)])
    inner = grad_normed * gain
    slope = jnp.mean(inner, axis=-1, keepdims=True)
    tilt = jnp.mean(inner * xhat, axis=-1, keepdims=True)
    grad_stream = grad_stream + (inner - slope - xhat * tilt) * factor
    return grad_stream, (grad_gate, grad_value, grad_mix, grad_out), norm_terms, kern_hat, grad_skip


def shards(tokens, lengths, cotangent, w_gate, w_value, w_mix, w_out, ln_gain, ln_bias, ssm_coef, ssm_rate, ssm_skip):
    dp = lax.axis_size("dp")
    count = lax.axis_size("seq")
    me = lax.axis_index("seq")
    rows, model = tokens.shape
    length = rows * count
    depth, in_rows, gate_width = w_gate.shape
    mix_rows = w_mix.shape[1]
    width = ssm_coef.shape[2]
    states = ssm_coef.shape[3]
    share = gate_width // (dp * count)

    waves_flat = jnp.asarray(wave_table(length))
    order = me ^ jnp.arange(count, dtype=jnp.int32)
    waves = jnp.take(waves_flat.reshape(2 * length, count, rows), order, axis=1).reshape(2 * length, length)
    positions = (order[:, None] * rows + jnp.arange(rows, dtype=jnp.int32)[None, :]).reshape(length)
    keep = (positions < lengths[0]).astype(F32)[:, None]

    def by_column(weight):
        cut = weight.reshape(depth, weight.shape[1], dp, count, share)
        return cut.transpose(3, 0, 1, 2, 4).reshape(count, depth, weight.shape[1], width)

    sent_value = w_value.reshape(depth, in_rows, 2, count, width).transpose(3, 0, 2, 1, 4)
    sent_value = sent_value.reshape(count, depth, 2 * in_rows, width)
    norm_rows = jnp.stack([ln_gain, ln_bias], 1).reshape(2 * depth, in_rows)
    sent = jnp.concatenate([by_column(w_gate), sent_value, by_column(w_mix)], 2)
    sent = sent.reshape(count, depth * (3 * in_rows + mix_rows), width)
    norm_pad = jnp.pad(norm_rows, ((0, 16 - 2 * depth), (0, width - in_rows)))
    sent = jnp.concatenate([sent, jnp.broadcast_to(norm_pad, (count,) + norm_pad.shape)], 1)
    came = lax.all_to_all(sent, "seq", 0, 0, tiled=True)
    norm_came = came[:, depth * (3 * in_rows + mix_rows) :]
    came = came[:, : depth * (3 * in_rows + mix_rows)].reshape(count, depth, 3 * in_rows + mix_rows, width)

    def gather_dp(block):
        return lax.all_gather(block, "dp", axis=0)

    def early_block(layer):
        block = came[:, layer, : 3 * in_rows].reshape(count, 3, in_rows, width)
        return block.transpose(1, 0, 2, 3).reshape(3 * count * in_rows, width)

    def late_block(layer):
        mix = came[:, layer, 3 * in_rows :].reshape(count * mix_rows, width)
        out = w_out[layer].reshape(mix_rows, model // width, width).transpose(1, 0, 2).reshape(-1, width)
        return jnp.concatenate([mix, out], 0)

    got_norm = None
    weights = []
    for layer in range(depth):
        early = early_block(layer)
        late = late_block(layer)
        n_early = early.shape[0]
        n_mix = count * mix_rows
        if layer == 0:
            early = jnp.concatenate([early, norm_came.reshape(count * 16, width)], 0)
            got = gather_dp(early)
            got_norm = got[:, n_early:].reshape(dp, count, 16, width)[:, :, : 2 * depth, :in_rows]
            got_norm = got_norm.transpose(2, 0, 1, 3).reshape(depth, 2, model).astype(F32)
            got_early = got[:, :n_early]
            got_late = gather_dp(late)
        else:
            got = gather_dp(jnp.concatenate([early, late], 0))
            got_early = got[:, :n_early]
            got_late = got[:, n_early:]
        got_early = got_early.reshape(dp, 3, count * in_rows, width)
        gate = got_early[:, 0].reshape(model, width)
        value = jnp.concatenate(
            [got_early[:, 1].reshape(model, width), got_early[:, 2].reshape(model, width)], 1
        )
        mix = got_late[:, :n_mix].reshape(count, width, width)
        mix = [lax.dynamic_index_in_dim(mix, order[m], 0, keepdims=False) for m in range(count)]
        out = got_late[:, n_mix:].reshape(dp, model // width, mix_rows, width)
        out = out.transpose(0, 2, 1, 3).reshape(dp * mix_rows, model)
        weights.append((gate, value, mix, out, got_norm[layer, 0], got_norm[layer, 1]))

    sign = jnp.concatenate([jnp.ones((width,), F32), -jnp.ones((width,), F32)])
    hats = []
    for layer in range(depth):
        kern = lag_kernels(
            ssm_coef[layer].reshape(2 * width, states), ssm_rate[layer].reshape(2 * width, states), length
        )
        both = dot(waves_flat, kern.astype(BF), 1, 1)
        hats.append((both[:length], both[length:] * sign))
    skips = ssm_skip.reshape(depth, 2 * width)

    stream = tokens.astype(F32)
    kept = []
    for layer in range(depth):
        stream, saved = run_layer(stream, keep, weights[layer], hats[layer], skips[layer], waves, count)
        kept.append(saved)

    grad_stream = cotangent.astype(F32)
    norm_grads = [None] * depth
    ssm_grads = [None] * depth
    shares = [None] * depth
    for layer in reversed(range(depth)):
        grad_stream, terms, norm_terms, kern_hat, grad_skip = back_layer(
            grad_stream, kept[layer], weights[layer], hats[layer], skips[layer], waves, count
        )
        norm_grads[layer] = norm_terms
        both = jnp.concatenate([kern_hat[0], kern_hat[1] * sign], 0).astype(BF)
        kern_grad = dot(both, waves_flat, 0, 0) * (1.0 / length)
        coef_grad, rate_grad = lag_grads(
            ssm_coef[layer].reshape(2 * width, states),
            ssm_rate[layer].reshape(2 * width, states),
            kern_grad,
            length,
        )
        ssm_grads[layer] = (coef_grad, rate_grad, grad_skip)
        grad_gate, grad_value, grad_mix, grad_out = terms
        out_rows = grad_out.astype(BF).reshape(dp, mix_rows, model // width, width).transpose(0, 2, 1, 3)
        mix_blocks = jnp.stack(grad_mix).astype(BF)
        mix_rows_all = jnp.take(mix_blocks, order, axis=0).reshape(dp, count * mix_rows, width)
        late = jnp.concatenate([mix_rows_all, out_rows.reshape(dp, -1, width)], 1)
        early = jnp.concatenate(
            [
                grad_gate.astype(BF).reshape(dp, 1, count * in_rows, width),
                grad_value.astype(BF).reshape(dp, count * in_rows, 2, width).transpose(0, 2, 1, 3),
            ],
            1,
        ).reshape(dp, 3 * count * in_rows, width)
        late = lax.psum_scatter(late, "dp", scatter_dimension=0, tiled=False)
        early = lax.psum_scatter(early, "dp", scatter_dimension=0, tiled=False)
        share_out = late[count * mix_rows :].reshape(model // width, mix_rows, width).transpose(1, 0, 2)
        share_out = share_out.reshape(mix_rows, model).astype(F32)
        back_mix = late[: count * mix_rows].reshape(count, mix_rows, width)
        back_early = early.reshape(3, count, in_rows, width).transpose(1, 0, 2, 3).reshape(count, 3 * in_rows, width)
        back = lax.all_to_all(jnp.concatenate([back_early, back_mix], 1), "seq", 0, 0, tiled=True)

        def columns(block, block_rows):
            cut = block.reshape(count, block_rows, dp, share).transpose(1, 2, 0, 3)
            return cut.reshape(block_rows, gate_width).astype(F32)

        share_gate = columns(back[:, :in_rows], in_rows)
        share_value = back[:, in_rows : 3 * in_rows].reshape(count, 2, in_rows, width).transpose(2, 1, 0, 3)
        share_value = share_value.reshape(in_rows, 2 * count * width).astype(F32)
        share_mix = columns(back[:, 3 * in_rows :], mix_rows)
        shares[layer] = (share_gate, share_value, share_mix, share_out)

    norm_all = jnp.stack(norm_grads).reshape(2 * depth, dp * count, in_rows).transpose(1, 0, 2)
    norm_sum = jnp.sum(
        lax.all_to_all(norm_all.reshape(dp * count, 2 * depth * in_rows), ("dp", "seq"), 0, 0, tiled=True), 0
    ).reshape(depth, 2, in_rows)
    coef_sum = lax.psum(jnp.stack([g[0] for g in ssm_grads]).astype(BF), "dp").astype(F32)
    rate_sum = lax.psum(jnp.stack([g[1] for g in ssm_grads]).astype(BF), "dp").astype(F32)
    skip_sum = lax.psum(jnp.stack([g[2] for g in ssm_grads]).astype(BF), "dp").astype(F32)
    stacked = [jnp.stack([shares[layer][member] for layer in range(depth)]) for member in range(4)]
    return (
        stream,
        grad_stream,
        stacked[0],
        stacked[1],
        stacked[2],
        stacked[3],
        norm_sum[:, 0],
        norm_sum[:, 1],
        coef_sum.reshape(ssm_coef.shape),
        rate_sum.reshape(ssm_rate.shape),
        skip_sum.reshape(ssm_skip.shape),
    )


def solution(mesh):
    in_specs = (
        P(("dp", "seq"), None),
        P("dp"),
        P(("dp", "seq"), None),
        P(None, ("dp", "seq"), None),
        P(None, ("dp", "seq"), None),
        P(None, ("dp", "seq"), None),
        P(None, ("dp", "seq"), None),
        P(None, ("dp", "seq")),
        P(None, ("dp", "seq")),
        P(None, None, "seq", None),
        P(None, None, "seq", None),
        P(None, None, "seq"),
    )
    out_specs = (
        P(("dp", "seq"), None),
        P(("dp", "seq"), None),
        P(None, ("dp", "seq"), None),
        P(None, ("dp", "seq"), None),
        P(None, ("dp", "seq"), None),
        P(None, ("dp", "seq"), None),
        P(None, ("dp", "seq")),
        P(None, ("dp", "seq")),
        P(None, None, "seq", None),
        P(None, None, "seq", None),
        P(None, None, "seq"),
    )
    return jax.shard_map(shards, mesh=mesh, in_specs=in_specs, out_specs=out_specs, check_vma=False)
```

```python
import numpy as np

import jax
import jax.numpy as jnp
from jax import lax
from jax.sharding import PartitionSpec as P

EPSILON = 1e-05
BF = jnp.bfloat16
F32 = jnp.float32
LAG_BLOCK = 128


def dot(left, right, left_dim, right_dim):
    return lax.dot_general(
        left, right, (((left_dim,), (right_dim,)), ((), ())), preferred_element_type=F32
    )


def wave_table(length):
    turns = 4 * length
    step = np.arange(length, dtype=np.int64)
    phase = ((2 * step[:, None] + 1) * step[None, :]) % turns
    angle = phase * (2.0 * np.pi / turns)
    return np.concatenate([np.cos(angle), np.sin(angle)], 0).astype(jnp.bfloat16)


def seq_pairs(count, bit):
    return [(i, i ^ bit) for i in range(count)]


def seq_gather(block, count):
    blocks = {0: block}
    bit = count // 2
    while bit:
        for member in list(blocks):
            blocks[member ^ bit] = lax.ppermute(blocks[member], "seq", seq_pairs(count, bit))
        bit //= 2
    return [blocks[m] for m in range(count)]


def seq_reduce(blocks, count):
    blocks = dict(enumerate(blocks))
    bit = 1
    while bit < count:
        for member in sorted(blocks, reverse=True):
            if member & bit:
                sent = blocks.pop(member).astype(BF)
                came = lax.ppermute(sent, "seq", seq_pairs(count, bit))
                blocks[member ^ bit] = blocks[member ^ bit] + came.astype(F32)
        bit *= 2
    return blocks[0]


def dp_pairs(count, bit):
    return [(i, i ^ bit) for i in range(count)]


def bits_of(count):
    return [1 << j for j in range(count.bit_length() - 1)]


def dp_gather(block, count, sequence):
    me = lax.axis_index("dp")
    for bit in sequence:
        other = lax.ppermute(block, "dp", dp_pairs(count, bit))
        upper = (me & bit) != 0
        block = jnp.stack([jnp.where(upper, other, block), jnp.where(upper, block, other)])
    axes = [sequence[::-1].index(bit) for bit in bits_of(count)[::-1]]
    rest = range(len(axes), block.ndim)
    block = block.transpose(*axes, *rest)
    return block.reshape((count,) + block.shape[len(axes) :])


def dp_reduce(blocks, count, sequence):
    me = lax.axis_index("dp")
    levels = bits_of(count)[::-1]
    blocks = blocks.reshape((2,) * len(levels) + blocks.shape[1:])
    for bit in sequence:
        axis = levels.index(bit)
        side = (me // bit) % 2
        sent = lax.dynamic_slice_in_dim(blocks, 1 - side, 1, axis).astype(BF)
        held = lax.dynamic_slice_in_dim(blocks, side, 1, axis)
        came = lax.ppermute(sent, "dp", dp_pairs(count, bit))
        blocks = (held.astype(F32) + came.astype(F32)).astype(BF)
    return blocks.reshape(blocks.shape[len(levels) :])


def dp_reduce_halves(blocks, count):
    bits = bits_of(count)
    middle = blocks.shape[1] // 32 * 16
    return jnp.concatenate(
        [
            dp_reduce(blocks[:, :middle], count, bits),
            dp_reduce(blocks[:, middle:], count, bits[1:] + bits[:1]),
        ],
        0,
    )


def gelu_parts(pre):
    share = 0.5 * (1.0 + lax.erf(pre * np.float32(np.sqrt(0.5))))
    slope = share + pre * (jnp.exp(-0.5 * pre * pre) * np.float32(1.0 / np.sqrt(2.0 * np.pi)))
    return pre * share, slope


def normalize(stream):
    centre = jnp.mean(stream, axis=-1, keepdims=True)
    centred = stream - centre
    spread = jnp.mean(centred * centred, axis=-1, keepdims=True)
    factor = lax.rsqrt(spread + EPSILON)
    return centred * factor, factor


def lag_factors(rates, length):
    block = min(LAG_BLOCK, length)
    far = jnp.exp(-rates[:, None, :] * (block * jnp.arange(length // block, dtype=F32))[None, :, None])
    near = jnp.exp(-rates[:, None, :] * jnp.arange(block, dtype=F32)[None, :, None])
    return far, near


def lag_kernels(coef, rates, length):
    far, near = lag_factors(rates, length)
    left = ((coef * rates)[:, None, :] * far).astype(BF)
    kern = lax.dot_general(
        left, near.astype(BF), (((2,), (2,)), ((0,), (0,))), preferred_element_type=F32
    )
    return kern.reshape(coef.shape[0], length)


def lag_grads(coef, rates, kern_grad, length):
    far, near = lag_factors(rates, length)
    block = near.shape[1]
    lags = jnp.arange(block, dtype=F32)[None, :, None]
    pair = jnp.concatenate([near, near * lags], axis=2).astype(BF)
    pieces = kern_grad.reshape(rates.shape[0], length // block, block).astype(BF)
    sums = lax.dot_general(pieces, pair, (((2,), (1,)), ((0,), (0,))), preferred_element_type=F32)
    states = rates.shape[1]
    plain = sums[:, :, :states]
    starts = (block * jnp.arange(length // block, dtype=F32))[None, :, None]
    total = jnp.sum(far * plain, axis=1)
    moment = jnp.sum(far * (starts * plain + sums[:, :, states:]), axis=1)
    return rates * total, coef * (total - rates * moment)


def spectrum_of(waves, series):
    both = dot(waves, series, 1, 0)
    half = both.shape[0] // 2
    return both[:half], both[half:]


def series_of(waves, cos_part, sin_part):
    half = cos_part.shape[0]
    both = jnp.concatenate([cos_part, sin_part], 0).astype(BF)
    return dot(waves, both, 0, 0) * (1.0 / half)


def run_layer(stream, keep, weights, kernel_hat, skip, waves, count):
    w_gate, w_value, w_mix, w_out, gain, bias = weights
    xhat, factor = normalize(stream)
    normed_own = (xhat * gain + bias).astype(BF)
    normed = jnp.concatenate(seq_gather(normed_own, count), 0)
    gate_act, gate_slope = gelu_parts(dot(normed, w_gate, 1, 0))
    value_act, value_slope = gelu_parts(dot(normed, w_value, 1, 0))
    values = (value_act * keep).astype(BF)
    value_slope = (value_slope * keep).astype(BF)
    x_cos, x_sin = spectrum_of(waves, values)
    k_cos, k_sin = kernel_hat
    mixes = series_of(waves, k_cos * x_cos - k_sin * x_sin, k_cos * x_sin + k_sin * x_cos)
    mixes = mixes + skip * values.astype(F32)
    width = mixes.shape[1] // 2
    product = (mixes[:, :width] * mixes[:, width:]).astype(BF)
    rows = stream.shape[0]
    products = []
    for member, came in enumerate(seq_gather(product, count)):
        pieces = came.reshape(count, rows, width)
        products.append(jnp.concatenate([pieces[m ^ member] for m in range(count)], 0))
    update = dot(products[0], w_mix[0], 1, 0)
    for member in range(1, count):
        update = update + dot(products[member], w_mix[member], 1, 0)
    mixed = (update * gate_act).astype(BF)
    partial = dot(mixed, w_out, 1, 0)
    result = stream + seq_reduce(
        [partial[m * rows : (m + 1) * rows] for m in range(count)], count
    )
    saved = (
        xhat,
        factor,
        normed,
        gate_act.astype(BF),
        (update * gate_slope).astype(BF),
        value_slope,
        values,
        (x_cos.astype(BF), x_sin.astype(BF)),
        mixes.astype(BF),
        products,
        mixed,
    )
    return result, saved


def back_layer(grad_stream, saved, weights, kernel_hat, skip, waves, count):
    w_gate, w_value, w_mix, w_out, gain, bias = weights
    xhat, factor, normed, gate_act, gate_back, value_slope, values, x_hat, mixes, products, mixed = saved
    rows = grad_stream.shape[0]
    out_low = jnp.concatenate(seq_gather(grad_stream.astype(BF), count), 0)
    grad_mixed = dot(out_low, w_out, 1, 1)
    grad_out = dot(mixed, out_low, 0, 0)
    update_low = (grad_mixed * gate_act.astype(F32)).astype(BF)
    gate_grad = (grad_mixed * gate_back.astype(F32)).astype(BF)
    width = products[0].shape[1]
    partials = []
    for member in range(count):
        part = dot(update_low, w_mix[member], 1, 1).reshape(count, rows, width)
        partials.append(jnp.concatenate([part[m ^ member] for m in range(count)], 0))
    product_low = seq_reduce(partials, count).astype(BF).astype(F32)
    grad_mix = [dot(products[member], update_low, 0, 0) for member in range(count)]
    mixes = mixes.astype(F32)
    back = jnp.concatenate([product_low * mixes[:, width:], product_low * mixes[:, :width]], 1)
    back_low = back.astype(BF)
    g_cos, g_sin = spectrum_of(waves, back_low)
    k_cos, k_sin = kernel_hat
    grad_values = series_of(waves, k_cos * g_cos + k_sin * g_sin, k_cos * g_sin - k_sin * g_cos)
    grad_values = grad_values + skip * back
    x_cos, x_sin = x_hat
    x_cos = x_cos.astype(F32)
    x_sin = x_sin.astype(F32)
    kern_hat = (g_cos * x_cos + g_sin * x_sin, g_sin * x_cos - g_cos * x_sin)
    grad_skip = jnp.sum(back * values.astype(F32), axis=0)
    value_grad = (grad_values.astype(BF).astype(F32) * value_slope.astype(F32)).astype(BF)
    grad_value = dot(normed, value_grad, 0, 0)
    grad_gate = dot(normed, gate_grad, 0, 0)
    partial = dot(value_grad, w_value, 1, 1) + dot(gate_grad, w_gate, 1, 1)
    grad_normed = seq_reduce([partial[m * rows : (m + 1) * rows] for m in range(count)], count)
    norm_terms = jnp.stack([jnp.sum(grad_normed * xhat, 0), jnp.sum(grad_normed, 0)])
    inner = grad_normed * gain
    slope = jnp.mean(inner, axis=-1, keepdims=True)
    tilt = jnp.mean(inner * xhat, axis=-1, keepdims=True)
    grad_stream = grad_stream + (inner - slope - xhat * tilt) * factor
    return grad_stream, (grad_gate, grad_value, grad_mix, grad_out), norm_terms, kern_hat, grad_skip


def shards(tokens, lengths, cotangent, w_gate, w_value, w_mix, w_out, ln_gain, ln_bias, ssm_coef, ssm_rate, ssm_skip):
    dp = lax.axis_size("dp")
    count = lax.axis_size("seq")
    me = lax.axis_index("seq")
    rows, model = tokens.shape
    length = rows * count
    depth, in_rows, gate_width = w_gate.shape
    mix_rows = w_mix.shape[1]
    width = ssm_coef.shape[2]
    states = ssm_coef.shape[3]
    share = gate_width // (dp * count)

    waves_flat = jnp.asarray(wave_table(length))
    order = me ^ jnp.arange(count, dtype=jnp.int32)
    waves = jnp.take(waves_flat.reshape(2 * length, count, rows), order, axis=1).reshape(2 * length, length)
    positions = (order[:, None] * rows + jnp.arange(rows, dtype=jnp.int32)[None, :]).reshape(length)
    keep = (positions < lengths[0]).astype(F32)[:, None]

    def by_column(weight):
        cut = weight.reshape(depth, weight.shape[1], dp, count, share)
        return cut.transpose(3, 0, 1, 2, 4).reshape(count, depth, weight.shape[1], width)

    sent_value = w_value.reshape(depth, in_rows, 2, count, width).transpose(3, 0, 2, 1, 4)
    sent_value = sent_value.reshape(count, depth, 2 * in_rows, width)
    norm_rows = jnp.stack([ln_gain, ln_bias], 1).reshape(2 * depth, in_rows)
    sent = jnp.concatenate([by_column(w_gate), sent_value, by_column(w_mix)], 2)
    sent = sent.reshape(count, depth * (3 * in_rows + mix_rows), width)
    norm_pad = jnp.pad(norm_rows, ((0, 16 - 2 * depth), (0, width - in_rows)))
    sent = jnp.concatenate([sent, jnp.broadcast_to(norm_pad, (count,) + norm_pad.shape)], 1)
    came = lax.all_to_all(sent, "seq", 0, 0, tiled=True)
    norm_came = came[:, depth * (3 * in_rows + mix_rows) :]
    came = came[:, : depth * (3 * in_rows + mix_rows)].reshape(count, depth, 3 * in_rows + mix_rows, width)

    def gather_dp(block):
        return lax.all_gather(block, "dp", axis=0)

    def early_block(layer):
        block = came[:, layer, : 3 * in_rows].reshape(count, 3, in_rows, width)
        return block.transpose(1, 0, 2, 3).reshape(3 * count * in_rows, width)

    def late_block(layer):
        mix = came[:, layer, 3 * in_rows :].reshape(count * mix_rows, width)
        out = w_out[layer].reshape(mix_rows, model // width, width).transpose(1, 0, 2).reshape(-1, width)
        return jnp.concatenate([mix, out], 0)

    got_norm = None
    weights = []
    for layer in range(depth):
        early = early_block(layer)
        late = late_block(layer)
        n_early = early.shape[0]
        n_mix = count * mix_rows
        if layer == 0:
            early = jnp.concatenate([early, norm_came.reshape(count * 16, width)], 0)
            bits = bits_of(dp)
            middle = early.shape[0] // 32 * 16
            got = jnp.concatenate(
                [
                    dp_gather(early[:middle], dp, bits[:0:-1] + bits[:1]),
                    dp_gather(early[middle:], dp, bits[:1] + bits[:0:-1]),
                ],
                1,
            )
            got, late = lax.optimization_barrier((got, late))
            got_norm = got[:, n_early:].reshape(dp, count, 16, width)[:, :, : 2 * depth, :in_rows]
            got_norm = got_norm.transpose(2, 0, 1, 3).reshape(depth, 2, model).astype(F32)
            got_early = got[:, :n_early]
            got_late = gather_dp(late)
        else:
            got = gather_dp(jnp.concatenate([early, late], 0))
            got_early = got[:, :n_early]
            got_late = got[:, n_early:]
        got_early = got_early.reshape(dp, 3, count * in_rows, width)
        gate = got_early[:, 0].reshape(model, width)
        value = jnp.concatenate(
            [got_early[:, 1].reshape(model, width), got_early[:, 2].reshape(model, width)], 1
        )
        mix = got_late[:, :n_mix].reshape(count, width, width)
        mix = [lax.dynamic_index_in_dim(mix, order[m], 0, keepdims=False) for m in range(count)]
        out = got_late[:, n_mix:].reshape(dp, model // width, mix_rows, width)
        out = out.transpose(0, 2, 1, 3).reshape(dp * mix_rows, model)
        weights.append((gate, value, mix, out, got_norm[layer, 0], got_norm[layer, 1]))

    sign = jnp.concatenate([jnp.ones((width,), F32), -jnp.ones((width,), F32)])
    hats = []
    for layer in range(depth):
        kern = lag_kernels(
            ssm_coef[layer].reshape(2 * width, states), ssm_rate[layer].reshape(2 * width, states), length
        )
        both = dot(waves_flat, kern.astype(BF), 1, 1)
        hats.append((both[:length], both[length:] * sign))
    skips = ssm_skip.reshape(depth, 2 * width)

    stream = tokens.astype(F32)
    kept = []
    for layer in range(depth):
        stream, saved = run_layer(stream, keep, weights[layer], hats[layer], skips[layer], waves, count)
        kept.append(saved)

    grad_stream = cotangent.astype(F32)
    norm_grads = [None] * depth
    ssm_grads = [None] * depth
    shares = [None] * depth
    parts = [None] * depth
    for layer in reversed(range(depth)):
        grad_stream, terms, norm_terms, kern_hat, grad_skip = back_layer(
            grad_stream, kept[layer], weights[layer], hats[layer], skips[layer], waves, count
        )
        norm_grads[layer] = norm_terms
        both = jnp.concatenate([kern_hat[0], kern_hat[1] * sign], 0).astype(BF)
        kern_grad = dot(both, waves_flat, 0, 0) * (1.0 / length)
        coef_grad, rate_grad = lag_grads(
            ssm_coef[layer].reshape(2 * width, states),
            ssm_rate[layer].reshape(2 * width, states),
            kern_grad,
            length,
        )
        ssm_grads[layer] = (coef_grad, rate_grad, grad_skip)
        grad_gate, grad_value, grad_mix, grad_out = terms
        out_rows = grad_out.astype(BF).reshape(dp, mix_rows, model // width, width).transpose(0, 2, 1, 3)
        mix_blocks = jnp.stack(grad_mix).astype(BF)
        mix_rows_all = jnp.take(mix_blocks, order, axis=0).reshape(dp, count * mix_rows, width)
        late = jnp.concatenate([mix_rows_all, out_rows.reshape(dp, -1, width)], 1)
        early = jnp.concatenate(
            [
                grad_gate.astype(BF).reshape(dp, 1, count * in_rows, width),
                grad_value.astype(BF).reshape(dp, count * in_rows, 2, width).transpose(0, 2, 1, 3),
            ],
            1,
        ).reshape(dp, 3 * count * in_rows, width)
        if layer:
            held = lax.psum_scatter(jnp.concatenate([early, late], 1), "dp", scatter_dimension=0, tiled=False)
            parts[layer] = held
        else:
            if depth > 1:
                early, parts[depth - 1] = lax.optimization_barrier((early, parts[depth - 1]))
            late = dp_reduce(late, dp, bits_of(dp))
            early = dp_reduce_halves(early, dp)
            parts[layer] = jnp.concatenate([early, late], 0)
    for layer in range(depth):
        early = parts[layer][: 3 * count * in_rows]
        late = parts[layer][3 * count * in_rows :]
        share_out = late[count * mix_rows :].reshape(model // width, mix_rows, width).transpose(1, 0, 2)
        share_out = share_out.reshape(mix_rows, model).astype(F32)
        back_mix = late[: count * mix_rows].reshape(count, mix_rows, width)
        back_early = early.reshape(3, count, in_rows, width).transpose(1, 0, 2, 3).reshape(count, 3 * in_rows, width)
        back = lax.all_to_all(jnp.concatenate([back_early, back_mix], 1), "seq", 0, 0, tiled=True)

        def columns(block, block_rows):
            cut = block.reshape(count, block_rows, dp, share).transpose(1, 2, 0, 3)
            return cut.reshape(block_rows, gate_width).astype(F32)

        share_gate = columns(back[:, :in_rows], in_rows)
        share_value = back[:, in_rows : 3 * in_rows].reshape(count, 2, in_rows, width).transpose(2, 1, 0, 3)
        share_value = share_value.reshape(in_rows, 2 * count * width).astype(F32)
        share_mix = columns(back[:, 3 * in_rows :], mix_rows)
        shares[layer] = (share_gate, share_value, share_mix, share_out)

    norm_all = jnp.stack(norm_grads).reshape(2 * depth, dp * count, in_rows).transpose(1, 0, 2)
    norm_sum = jnp.sum(
        lax.all_to_all(norm_all.reshape(dp * count, 2 * depth * in_rows), ("dp", "seq"), 0, 0, tiled=True), 0
    ).reshape(depth, 2, in_rows)
    own = 2 * width // dp
    ssm_rows = []
    for coef_grad, rate_grad, grad_skip in ssm_grads:
        ssm_rows.append(jnp.concatenate([coef_grad, rate_grad], 1).reshape(dp, own, 2 * states))
        skip_row = jnp.pad(grad_skip.reshape(dp, own), ((0, 0), (0, -own % (2 * states))))
        ssm_rows.append(skip_row.reshape(dp, -1, 2 * states))
    ssm_rows = jnp.concatenate(ssm_rows, 1)
    ssm_rows = jnp.pad(ssm_rows, ((0, 0), (0, -ssm_rows.shape[1] % 16), (0, 0))).astype(BF)
    ssm_sum = dp_gather(dp_reduce(ssm_rows, dp, bits_of(dp)), dp, bits_of(dp)[::-1]).astype(F32)
    each = own + -(-own // (2 * states))
    ssm_sum = ssm_sum[:, : depth * each].reshape(dp, depth, each, 2 * states)
    coef_sum = ssm_sum[:, :, :own, :states].transpose(1, 0, 2, 3)
    rate_sum = ssm_sum[:, :, :own, states:].transpose(1, 0, 2, 3)
    skip_sum = ssm_sum[:, :, own:].reshape(dp, depth, -1)[:, :, :own].transpose(1, 0, 2)
    stacked = [jnp.stack([shares[layer][member] for layer in range(depth)]) for member in range(4)]
    return (
        stream,
        grad_stream,
        stacked[0],
        stacked[1],
        stacked[2],
        stacked[3],
        norm_sum[:, 0],
        norm_sum[:, 1],
        coef_sum.reshape(ssm_coef.shape),
        rate_sum.reshape(ssm_rate.shape),
        skip_sum.reshape(ssm_skip.shape),
    )


def solution(mesh):
    in_specs = (
        P(("dp", "seq"), None),
        P("dp"),
        P(("dp", "seq"), None),
        P(None, ("dp", "seq"), None),
        P(None, ("dp", "seq"), None),
        P(None, ("dp", "seq"), None),
        P(None, ("dp", "seq"), None),
        P(None, ("dp", "seq")),
        P(None, ("dp", "seq")),
        P(None, None, "seq", None),
        P(None, None, "seq", None),
        P(None, None, "seq"),
    )
    out_specs = (
        P(("dp", "seq"), None),
        P(("dp", "seq"), None),
        P(None, ("dp", "seq"), None),
        P(None, ("dp", "seq"), None),
        P(None, ("dp", "seq"), None),
        P(None, ("dp", "seq"), None),
        P(None, ("dp", "seq")),
        P(None, ("dp", "seq")),
        P(None, None, "seq", None),
        P(None, None, "seq", None),
        P(None, None, "seq"),
    )
    return jax.shard_map(shards, mesh=mesh, in_specs=in_specs, out_specs=out_specs, check_vma=False)
```

```python
from functools import partial

import numpy as np

import jax
import jax.numpy as jnp
from jax import lax
from jax.experimental import pallas as pl
from jax.experimental.layout import Layout, with_layout_constraint
from jax.experimental.pallas import tpu as pltpu
from jax.sharding import PartitionSpec as P

EPSILON = 1e-05
BF = jnp.bfloat16
F32 = jnp.float32
LANES = 128
VMEM_BYTES = 56 * 2**20


def dot(left, right, left_dim, right_dim):
    return lax.dot_general(
        left, right, (((left_dim,), (right_dim,)), ((), ())), preferred_element_type=F32
    )


def wave_table(length):
    step = np.arange(length, dtype=np.int64)
    phase = ((2 * step[:, None] + 1) * step[None, :]) % (4 * length)
    angle = phase * (np.pi / (2 * length))
    return np.concatenate([np.cos(angle), np.sin(angle)], 0).astype(jnp.bfloat16)


def decay_tiles(rate):
    rows = lax.broadcasted_iota(jnp.int32, (8, LANES), 0).astype(F32)
    tiles = [jnp.exp(-rate * rows)]
    step = jnp.exp(-8.0 * jnp.broadcast_to(rate, (8, LANES)))
    while len(tiles) < LANES // 8:
        tiles = tiles + [tile * step for tile in tiles]
        step = step * step
    return tiles


def block_decays(rate, count):
    starts = lax.broadcasted_iota(jnp.int32, (count, LANES), 0).astype(F32) * float(LANES)
    return starts, jnp.exp(-rate * starts)


def spectra_kernel(unroll, rate_ref, coef_ref, sign_ref, wave_ref, *refs):
    cos_ref, sin_ref, kern_ref, flat_ref = refs[-4:]
    pairs = rate_ref.shape[0]
    length = wave_ref.shape[1]
    count = length // LANES
    lower = lax.broadcasted_iota(jnp.int32, (count, LANES), 1) < LANES // 2

    def pair(step, carry):
        for offset in range(unroll):
            index = step * unroll + offset
            rate = rate_ref[pl.ds(index, 1), :]
            near = jnp.concatenate(decay_tiles(rate), 0).astype(BF)
            far = block_decays(rate, count)[1] * (coef_ref[pl.ds(index, 1), :] * rate)
            left = jnp.concatenate([jnp.where(lower, far, 0.0), jnp.where(lower, 0.0, far)], 0)
            place = pl.ds(pl.multiple_of(index * 2 * count, 2 * count), 2 * count)
            kern_ref[place, :] = dot(left.astype(BF), near, 1, 1)
        return carry

    lax.fori_loop(0, pairs // unroll, pair, 0)
    for part in range(count):
        flat_ref[:, part * LANES : (part + 1) * LANES] = kern_ref[
            pl.ds(part, 2 * pairs, stride=count), :
        ].astype(BF)
    chunk = 256
    for part in range(length // chunk):
        rows = slice(part * chunk, (part + 1) * chunk)
        cos_ref[rows, :] = dot(wave_ref[rows, :], flat_ref[...], 1, 1).astype(BF)
        sines = dot(wave_ref[length + part * chunk : length + (part + 1) * chunk, :], flat_ref[...], 1, 1)
        sin_ref[rows, :] = (sines * sign_ref[...]).astype(BF)


def channel_block(channels):
    return 256 if channels % 256 == 0 else channels


def unroll_of(pairs):
    return 16 if pairs % 16 == 0 else 8


def spectra(coef, rate, sign, wave, part, earlier):
    channels = 2 * coef.shape[0]
    length = wave.shape[1]
    block = channel_block(channels)
    rows = pl.BlockSpec((block // 2, LANES), lambda j: (part, 0))
    lanes = pl.BlockSpec((length, block), lambda j: (0, part))
    shape = jax.ShapeDtypeStruct((length, channels), BF)
    return pl.pallas_call(
        partial(spectra_kernel, unroll_of(block // 2)),
        out_shape=(shape, shape),
        grid=(1,),
        in_specs=[
            rows,
            rows,
            pl.BlockSpec((1, block), lambda j: (0, part)),
            pl.BlockSpec((2 * length, length), lambda j: (0, 0)),
        ]
        + [pl.BlockSpec(memory_space=pl.ANY)] * len(earlier),
        out_specs=(lanes, lanes),
        scratch_shapes=[
            pltpu.VMEM((block * length // LANES, LANES), F32),
            pltpu.VMEM((block, length), BF),
        ],
        input_output_aliases={4 + j: j for j in range(len(earlier))},
        compiler_params=pltpu.CompilerParams(vmem_limit_bytes=VMEM_BYTES),
        cost_estimate=pl.CostEstimate(
            flops=12 * length * length * block,
            bytes_accessed=4 * length * length + 4 * length * block,
            transcendentals=0,
        ),
        name="spectra",
    )(rate, coef, sign, wave, *earlier)


def state_grads_kernel(
    unroll, rate_ref, coef_ref, cos_ref, sin_ref, wave_ref, coef_out, rate_out, turned_ref, kern_ref
):
    pairs = rate_ref.shape[0]
    length = wave_ref.shape[1]
    count = length // LANES
    lower = lax.broadcasted_iota(jnp.int32, (count, LANES), 1) < LANES // 2
    row = lax.broadcasted_iota(jnp.int32, (8, LANES), 0).astype(F32)
    turned_ref[:, :length] = cos_ref[...].T
    turned_ref[:, length:] = sin_ref[...].T
    chunk = 256
    for part in range(length // chunk):
        got = dot(turned_ref[...], wave_ref[:, part * chunk : (part + 1) * chunk], 1, 0)
        for side in range(chunk // LANES):
            place = pl.ds(part * (chunk // LANES) + side, 2 * pairs, stride=count)
            kern_ref[place, :] = got[:, side * LANES : (side + 1) * LANES]

    def pair(step, carry):
        for offset in range(unroll):
            index = step * unroll + offset
            rate = rate_ref[pl.ds(index, 1), :]
            coef = coef_ref[pl.ds(index, 1), :]
            tiles = decay_tiles(rate)
            near = jnp.concatenate(tiles, 0).astype(BF)
            lagged = jnp.concatenate([tile * (row + 8.0 * j) for j, tile in enumerate(tiles)], 0)
            place = pl.ds(pl.multiple_of(index * 2 * count, 2 * count), 2 * count)
            both = jnp.concatenate([near, lagged.astype(BF)], 1)
            got = dot(kern_ref[place, :].astype(BF), both, 1, 0)
            plain = jnp.where(lower, got[:count, :LANES], got[count:, :LANES])
            first = jnp.where(lower, got[:count, LANES:], got[count:, LANES:])
            starts, far = block_decays(rate, count)
            total = jnp.sum(far * plain, axis=0, keepdims=True)
            moment = jnp.sum(far * (starts * plain + first), axis=0, keepdims=True)
            coef_out[pl.ds(index, 1), :] = rate * total * (1.0 / length)
            rate_out[pl.ds(index, 1), :] = coef * (total - rate * moment) * (1.0 / length)
        return carry

    lax.fori_loop(0, pairs // unroll, pair, 0)


def state_grads(coef, rate, cosines, sines, wave):
    channels = 2 * coef.shape[0]
    length = wave.shape[1]
    block = channel_block(channels)
    rows = pl.BlockSpec((block // 2, LANES), lambda j: (j, 0))
    lanes = pl.BlockSpec((length, block), lambda j: (0, j))
    shape = jax.ShapeDtypeStruct(coef.shape, F32)
    return pl.pallas_call(
        partial(state_grads_kernel, unroll_of(block // 2)),
        out_shape=(shape, shape),
        grid=(channels // block,),
        in_specs=[rows, rows, lanes, lanes, pl.BlockSpec((2 * length, length), lambda j: (0, 0))],
        out_specs=(rows, rows),
        scratch_shapes=[
            pltpu.VMEM((block, 2 * length), BF),
            pltpu.VMEM((block * length // LANES, LANES), F32),
        ],
        compiler_params=pltpu.CompilerParams(vmem_limit_bytes=VMEM_BYTES),
        cost_estimate=pl.CostEstimate(
            flops=12 * length * length * channels,
            bytes_accessed=4 * length * length + 4 * length * channels,
            transcendentals=0,
        ),
        name="state_grads",
    )(rate, coef, cosines, sines, wave)


def pairs_of(count, bit):
    return [(i, i ^ bit) for i in range(count)]


def seq_gather(block, count, wait):
    blocks = {0: block}
    bit = count // 2
    while bit:
        for member in list(blocks):
            blocks[member ^ bit] = lax.ppermute(blocks[member], "seq", pairs_of(count, bit))
        if bit == count // 2:
            blocks[bit], wait = together(blocks[bit], wait)
        bit //= 2
    return [blocks[m] for m in range(count)], wait


def seq_rows(block, count, wait):
    whole, wait = gather_bits(block, "seq", count, far_first(count), wait)
    return row_major(whole.reshape(count * block.shape[0], block.shape[1])), wait


def seq_reduce(blocks, count):
    blocks = dict(enumerate(blocks))
    bit = 1
    while bit < count:
        for member in sorted(blocks, reverse=True):
            if member & bit:
                sent = blocks.pop(member).astype(BF)
                came = lax.ppermute(sent, "seq", pairs_of(count, bit))
                blocks[member ^ bit] = blocks[member ^ bit] + came.astype(F32)
        bit *= 2
    return blocks[0]


def seq_reduce_rows(whole, count):
    return reduce_bits(whole.reshape(count, -1, whole.shape[1]), "seq", count, bits_of(count), F32)


def row_major(array):
    return with_layout_constraint(array, Layout(tuple(range(array.ndim))))


def bits_of(count):
    return [1 << j for j in range(count.bit_length() - 1)]


def far_first(count):
    return bits_of(count)[::-1]


def y_first(count):
    return bits_of(count)


def z_first(count):
    return bits_of(count)[1:] + bits_of(count)[:1]


def swap(block, axis, count, bit):
    return lax.ppermute(block, axis, pairs_of(count, bit))


def join(block, other, axis, bit, done):
    upper = (lax.axis_index(axis) & bit) != 0
    pair = [jnp.where(upper, other, block), jnp.where(upper, block, other)]
    return jnp.stack(pair, done.index(bit))


def gather_bits(block, axis, count, sequence, wait=()):
    done = []
    for bit in sequence:
        other = swap(block, axis, count, bit)
        if not done:
            other, wait = together(other, wait)
        done = sorted(done + [bit], reverse=True)
        block = join(block, other, axis, bit, done)
    return block.reshape((count,) + block.shape[len(done) :]), wait


def cut_half(blocks, axis, count, bit):
    level = far_first(count).index(bit)
    side = (lax.axis_index(axis) // bit) % 2
    sent = lax.dynamic_slice_in_dim(blocks, 1 - side, 1, level).astype(BF)
    return lax.dynamic_slice_in_dim(blocks, side, 1, level), sent


def add_half(held, came, kind):
    return (held.astype(F32) + came.astype(F32)).astype(kind)


def bit_blocks(blocks, count):
    return blocks.reshape((2,) * len(bits_of(count)) + blocks.shape[1:])


def reduce_bits(blocks, axis, count, sequence, kind):
    blocks = bit_blocks(blocks, count)
    for bit in sequence:
        held, sent = cut_half(blocks, axis, count, bit)
        blocks = add_half(held, swap(sent, axis, count, bit), kind)
    return blocks.reshape(blocks.shape[len(bits_of(count)) :])


def together(*arrays):
    return lax.optimization_barrier(arrays)


def gelu_parts(pre):
    share = 0.5 * (1.0 + lax.erf(pre * np.float32(np.sqrt(0.5))))
    slope = share + pre * (jnp.exp(-0.5 * pre * pre) * np.float32(1.0 / np.sqrt(2.0 * np.pi)))
    return pre * share, slope


def normalize(stream):
    centre = jnp.mean(stream, axis=-1, keepdims=True)
    centred = stream - centre
    spread = jnp.mean(centred * centred, axis=-1, keepdims=True)
    factor = lax.rsqrt(spread + EPSILON)
    return centred * factor, factor


def turned(spectrum):
    return jnp.stack([-spectrum[1], spectrum[0]])


def run_layer(stream, keep, early, late, hat, skip, tables, count, filler):
    w_value, gain, bias = early
    waves, waves_back = tables
    length = waves.shape[1]
    xhat, factor = normalize(stream)
    own, made = filler[0]((xhat * gain + bias).astype(BF))
    normed, made = seq_rows(own, count, made)
    value_act, value_slope = gelu_parts(dot(normed, w_value, 1, 0))
    values = (value_act * keep).astype(BF)
    value_slope = (value_slope * keep).astype(BF)
    values, value_slope = together(values, value_slope)
    x_hat = dot(waves, values, 1, 0).astype(BF)
    k_cos, k_sin = hat
    x_cos, x_sin = x_hat[:length].astype(F32), x_hat[length:].astype(F32)
    y_hat = jnp.concatenate([k_cos * x_cos - k_sin * x_sin, k_cos * x_sin + k_sin * x_cos], 0).astype(BF)
    mixes = dot(waves_back, y_hat, 1, 0) * (1.0 / length) + skip * values.astype(F32)
    width = mixes.shape[1] // 2
    product = (mixes[:, :width] * mixes[:, width:]).astype(BF)
    product, mixes = together(product, mixes.astype(BF))
    product, made = filler[1](product, made)
    products, made = seq_gather(product, count, made)
    w_gate, w_mix, w_out = late
    gate_act, gate_slope = gelu_parts(dot(normed, w_gate, 1, 0))
    update = dot(products[0], w_mix[0], 1, 0)
    for member in range(1, count):
        update = update + dot(products[member], w_mix[member], 1, 0)
    mixed = (update * gate_act).astype(BF)
    gate_back = (update * gate_slope).astype(BF)
    mixed, gate_act, gate_back = together(mixed, gate_act.astype(BF), gate_back)
    result = stream + seq_reduce_rows(dot(mixed, w_out, 1, 0), count)
    saved = (
        xhat,
        factor,
        normed,
        gate_act,
        gate_back,
        value_slope,
        values,
        x_hat,
        mixes,
        products,
        mixed,
    )
    return result, saved, made


def back_gate(grad_stream, saved, late, count, wait):
    w_gate, w_mix, w_out = late
    xhat, factor, normed, gate_act, gate_back, value_slope, values, x_hat, mixes, products, mixed = saved
    out_low, wait = seq_rows(grad_stream, count, wait)
    grad_mixed = dot(out_low, w_out, 1, 1)
    update_low = (grad_mixed * gate_act.astype(F32)).astype(BF)
    gate_grad = (grad_mixed * gate_back.astype(F32)).astype(BF)
    update_low, gate_grad = together(update_low, gate_grad)
    width = products[0].shape[1]
    model = out_low.shape[1]
    product_low = seq_reduce([dot(update_low, w_mix[m], 1, 1) for m in range(count)], count)
    grad_out = [
        dot(mixed, out_low[:, j * width : (j + 1) * width], 0, 0).astype(BF) for j in range(model // width)
    ]
    grad_mix = [dot(products[m], update_low, 0, 0).astype(BF) for m in range(count)]
    grad_gate = dot(normed, gate_grad, 0, 0).astype(BF)
    gate_part = dot(gate_grad, w_gate, 1, 1)
    return product_low.astype(BF), gate_part, (grad_gate, grad_mix, grad_out), wait


def back_convolution(product_low, saved, hat, skip, tables):
    xhat, factor, normed, gate_act, gate_back, value_slope, values, x_hat, mixes, products, mixed = saved
    waves, waves_back = tables
    length = waves.shape[1]
    width = product_low.shape[1]
    product_low = product_low.astype(F32)
    mixes = mixes.astype(F32)
    back = jnp.concatenate([product_low * mixes[:, width:], product_low * mixes[:, :width]], 1).astype(BF)
    g_hat = dot(waves, back, 1, 0).astype(BF)
    k_cos, k_sin = hat
    g_cos, g_sin = g_hat[:length].astype(F32), g_hat[length:].astype(F32)
    y_hat = jnp.concatenate([k_cos * g_cos + k_sin * g_sin, k_cos * g_sin - k_sin * g_cos], 0).astype(BF)
    grad_values = dot(waves_back, y_hat, 1, 0) * (1.0 / length) + skip * back.astype(F32)
    x_cos, x_sin = x_hat[:length].astype(F32), x_hat[length:].astype(F32)
    sign = jnp.concatenate([jnp.ones((width,), F32), -jnp.ones((width,), F32)])
    kern_hat = (
        (g_cos * x_cos + g_sin * x_sin).astype(BF),
        ((g_sin * x_cos - g_cos * x_sin) * sign).astype(BF),
    )
    grad_skip = jnp.sum(back.astype(F32) * values.astype(F32), axis=0)
    value_grad = (grad_values.astype(BF).astype(F32) * value_slope.astype(F32)).astype(BF)
    return value_grad, kern_hat, grad_skip


def back_norm(grad_stream, grad_normed, saved, gain):
    xhat, factor = saved[:2]
    norm_terms = jnp.stack([jnp.sum(grad_normed * xhat, 0), jnp.sum(grad_normed, 0)])
    inner = grad_normed * gain
    slope = jnp.mean(inner, axis=-1, keepdims=True)
    tilt = jnp.mean(inner * xhat, axis=-1, keepdims=True)
    return grad_stream + (inner - slope - xhat * tilt) * factor, norm_terms


def shards(tokens, lengths, cotangent, w_gate, w_value, w_mix, w_out, ln_gain, ln_bias, ssm_coef, ssm_rate, ssm_skip):
    dp = lax.axis_size("dp")
    count = lax.axis_size("seq")
    rows, model = tokens.shape
    length = rows * count
    depth, in_rows, gate_width = w_gate.shape
    mix_rows = w_mix.shape[1]
    width = ssm_coef.shape[2]
    states = ssm_coef.shape[3]
    share = gate_width // (dp * count)
    out_parts = model // width
    order = [lax.axis_index("seq") ^ m for m in range(count)]
    keep = (jnp.arange(length, dtype=jnp.int32) < lengths[0]).astype(F32)[:, None]
    table = wave_table(length)
    waves = jnp.asarray(table)
    tables = (waves, jnp.asarray(np.ascontiguousarray(table.T)))

    def by_column(weight):
        cut = weight.reshape(weight.shape[0], dp, count, share)
        return cut.transpose(2, 0, 1, 3).reshape(count, weight.shape[0], width)

    def value_columns(layer):
        cut = w_value[layer].reshape(in_rows, 2, count, width).transpose(2, 1, 0, 3)
        return cut.reshape(count, 2 * in_rows, width)

    norm_rows = jnp.stack([ln_gain, ln_bias], 1).reshape(2 * depth, in_rows)
    norm_rows = jnp.pad(norm_rows, ((0, 16 - 2 * depth), (0, width - in_rows)))
    first = jnp.concatenate([value_columns(0), jnp.broadcast_to(norm_rows, (count,) + norm_rows.shape)], 1)
    first = lax.all_to_all(first, "seq", 0, 0, tiled=True)
    pieces = [by_column(w_gate[0]), by_column(w_mix[0])]
    for layer in range(1, depth):
        pieces += [value_columns(layer), by_column(w_gate[layer]), by_column(w_mix[layer])]
    sizes = [piece.shape[1] for piece in pieces]
    rest = lax.all_to_all(jnp.concatenate(pieces, 1), "seq", 0, 0, tiled=True)
    rest = [piece for piece in jnp.split(rest, np.cumsum(sizes)[:-1].tolist(), axis=1)]

    coefs = ssm_coef.reshape(depth, width, 2 * states)
    rates = ssm_rate.reshape(depth, width, 2 * states)
    skips = ssm_skip.reshape(depth, 2 * width)
    sign = jnp.concatenate([jnp.ones((1, width), F32), -jnp.ones((1, width), F32)], 1)
    table_parts = 2 * width // channel_block(2 * width)

    def make_tables(layer, parts_made, hat, tie):
        rate, tie = together(rates[layer], tie)
        for part in parts_made:
            hat = spectra(coefs[layer], rate, sign, waves, part, hat)
        return hat, tie

    def flat(piece):
        return piece.reshape(-1, width)

    def value_sides(piece):
        return [flat(piece[:, side * in_rows : (side + 1) * in_rows]) for side in range(2)]

    def out_sides(layer):
        return [w_out[layer][:, j * width : (j + 1) * width] for j in range(out_parts)]

    norm_piece = first[:, 2 * in_rows :, :in_rows].transpose(1, 0, 2).reshape(16, count * in_rows)
    norm_piece = jnp.pad(norm_piece, ((0, 0), (0, -(count * in_rows) % width)))
    sides = value_sides(first)
    n_in = count * in_rows
    pair = [jnp.concatenate([sides[0], flat(norm_piece)], 0), sides[1]]
    paths = [far_first(dp), y_first(dp)[:1] + far_first(dp)[:-1]]
    late_block = jnp.concatenate([flat(rest[0]), flat(rest[1])] + out_sides(0), 0)
    done = [[], []]
    hat = ()
    for step in range(len(bits_of(dp))):
        others = [swap(block, "dp", dp, path[step]) for block, path in zip(pair, paths)]
        if step < table_parts:
            hat, pair = make_tables(0, [step], hat, pair)
            others, hat = together(others, hat)
        if step == 0:
            others, late_block = together(others, late_block)
        for j in range(2):
            done[j] = sorted(done[j] + [paths[j][step]], reverse=True)
            pair[j] = join(pair[j], others[j], "dp", paths[j][step], done[j])
    hat, pair = make_tables(0, range(len(bits_of(dp)), table_parts), hat, pair)
    hats = [hat]
    side_a, side_b = [block.reshape((dp,) + block.shape[-2:]) for block in pair]
    norms = side_a[:, n_in:].reshape(dp, 16, -1)[:, : 2 * depth, :n_in]
    norms = norms.transpose(1, 0, 2).reshape(depth, 2, model).astype(F32)

    def value_weight(side_a, side_b):
        return jnp.concatenate([side_a.reshape(model, width), side_b.reshape(model, width)], 1)

    def mix_weight(block):
        block = block.reshape(count, width, width)
        return [lax.dynamic_index_in_dim(block, order[m], 0, keepdims=False) for m in range(count)]

    def out_weight(block):
        cut = block.reshape(dp, out_parts, mix_rows, width).transpose(0, 2, 1, 3)
        return cut.reshape(dp * mix_rows, model)

    early = [(value_weight(side_a[:, :n_in], side_b), norms[0, 0], norms[0, 1])]
    got = lax.all_gather(late_block, "dp", axis=0)
    gate, mix, out = jnp.split(got, [n_in, n_in + count * mix_rows], axis=1)
    late = [(gate.reshape(model, width), mix_weight(mix), out_weight(out))]
    for layer in range(1, depth):
        value, gate, mix = rest[3 * layer - 1 : 3 * layer + 2]
        block = jnp.concatenate(value_sides(value) + [flat(gate), flat(mix)] + out_sides(layer), 0)
        got = lax.all_gather(block, "dp", axis=0)
        cuts = np.cumsum([n_in, n_in, n_in, count * mix_rows]).tolist()
        side_a, side_b, gate, mix, out = jnp.split(got, cuts, axis=1)
        early.append((value_weight(side_a, side_b), norms[layer, 0], norms[layer, 1]))
        late.append((gate.reshape(model, width), mix_weight(mix), out_weight(out)))

    stream = tokens.astype(F32)
    kept = []
    for layer in range(depth):
        if layer + 1 < depth:
            cut = min(2, table_parts)
            filler = (
                lambda own: make_tables(layer + 1, range(cut), (), own)[::-1],
                lambda product, made: make_tables(layer + 1, range(cut, table_parts), made, product)[::-1],
            )
        else:
            filler = (lambda own: (own, ()), lambda product, made: (product, made))
        stream, saved, made = run_layer(
            stream, keep, early[layer], late[layer], hats[layer], skips[layer], tables, count, filler
        )
        kept.append(saved)
        hats.append(made)

    def natural(blocks):
        whole = jnp.zeros((count,) + blocks[0].shape, blocks[0].dtype)
        for member, block in enumerate(blocks):
            whole = lax.dynamic_update_index_in_dim(whole, block, order[member], 0)
        return whole

    grad_stream = cotangent.astype(F32)
    norm_grads = [None] * depth
    ssm_grads = [None] * depth
    held = [None] * depth
    whole, kern_hat = None, None
    for layer in reversed(range(depth)):
        low = grad_stream.astype(BF)
        wait = ()
        if kern_hat is not None:
            low, whole, kern_hat = together(low, whole, kern_hat)
            held[layer + 1] = lax.psum_scatter(whole, "dp", scatter_dimension=0, tiled=False)
            wait = state_grads(coefs[layer + 1], rates[layer + 1], *kern_hat, waves)
        product_low, gate_part, terms, wait = back_gate(low, kept[layer], late[layer], count, wait)
        if kern_hat is not None:
            ssm_grads[layer + 1] += wait
        grad_gate, grad_mix, grad_out = terms
        mix = natural(grad_mix).reshape(dp, count * mix_rows, width)
        others = [grad_gate.reshape(dp, n_in, width)] + [g.reshape(dp, mix_rows, width) for g in grad_out]
        others = jnp.concatenate(others, 1)
        if not layer:
            paths = [y_first(dp), z_first(dp)]
            moving = [cut_half(bit_blocks(b, dp), "dp", dp, path[0]) for b, path in zip((mix, others), paths)]
            product_low, moving = together(product_low, moving)
            moving = [(pair[0], swap(pair[1], "dp", dp, path[0])) for pair, path in zip(moving, paths)]
        value_grad, kern_hat, grad_skip = back_convolution(product_low, kept[layer], hats[layer], skips[layer], tables)
        ssm_grads[layer] = (grad_skip,)
        normed = kept[layer][2]
        if not layer:
            value_grad, moving = together(value_grad, moving)
            moving = [cut_half(add_half(*pair, BF), "dp", dp, path[1]) for pair, path in zip(moving, paths)]
        values = [dot(normed, value_grad[:, j * width : (j + 1) * width], 0, 0).astype(BF) for j in range(2)]
        values = [g.reshape(dp, n_in, width) for g in values]
        parts = dot(value_grad, early[layer][0], 1, 1) + gate_part
        if layer:
            grad_normed = reduce_bits(
                parts.reshape(count, rows, model), "seq", count, bits_of(count), F32
            )
            whole = jnp.concatenate([mix, others] + values, 1)
        else:
            moving += [cut_half(bit_blocks(g, dp), "dp", dp, path[0]) for g, path in zip(values, paths)]
            paths = [path[1:] for path in paths] + paths
            sums = bit_blocks(parts.reshape(count, rows, model), count)
            for step, bit in enumerate(bits_of(count)):
                held_rows, sent = cut_half(sums, "seq", count, bit)
                if step == 1:
                    sent, moving, kern_hat = together(sent, moving, kern_hat)
                    moving = [(pair[0], swap(pair[1], "dp", dp, path[0])) for pair, path in zip(moving, paths)]
                    came = swap(sent, "seq", count, bit)
                    last = state_grads(coefs[0], rates[0], *kern_hat, waves)
                    came, moving, last = together(came, moving, last)
                    ssm_grads[0] += last
                else:
                    came = swap(sent, "seq", count, bit)
                sums = add_half(held_rows, came, F32)
            grad_normed = sums.reshape(rows, model)
        grad_stream, norm_grads[layer] = back_norm(grad_stream, grad_normed, kept[layer], early[layer][1])

    own = width // dp
    both = 2 * states
    skip_rows = jnp.stack([g[0].reshape(dp, 2 * own) for g in ssm_grads], 1)
    skip_rows = jnp.pad(skip_rows, ((0, 0), (0, 16 - depth), (0, -2 * own % both))).reshape(dp, -1, both)
    states_all = jnp.stack([g[j].reshape(dp, own, both) for g in ssm_grads for j in (1, 2)], 1).astype(BF)
    ssm_rows = jnp.concatenate([states_all.reshape(dp, 2 * depth * own, both), skip_rows.astype(BF)], 1)

    sums = [add_half(*pair, BF) for pair in moving] + [bit_blocks(ssm_rows, dp)]
    paths = [path[1:] for path in paths] + [y_first(dp)]
    while any(paths):
        active = [j for j, path in enumerate(paths) if path]
        pairs = [cut_half(sums[j], "dp", dp, paths[j][0]) for j in active]
        pairs = lax.optimization_barrier(pairs)
        pairs = [(pair[0], swap(pair[1], "dp", dp, paths[j][0])) for j, pair in zip(active, pairs)]
        pairs = lax.optimization_barrier(pairs)
        for j, pair in zip(active, pairs):
            sums[j] = add_half(*pair, BF)
            paths[j] = paths[j][1:]
    sums = [block.reshape(block.shape[-2:]) for block in sums]
    held[0] = jnp.concatenate(sums[:4], 0)
    ssm_sum = gather_bits(sums[4], "dp", dp, far_first(dp))[0].astype(F32)
    for layer in range(depth):
        cuts = np.cumsum([count * mix_rows, n_in, out_parts * mix_rows, n_in]).tolist()
        mix, gate, outs, side_a, side_b = jnp.split(held[layer], cuts, axis=0)
        held[layer] = ([side_a, side_b], gate, mix, outs)

    pieces = []
    for layer in range(depth):
        values, gate, mix, outs = held[layer]
        pieces += [gate.reshape(count, in_rows, width), mix.reshape(count, mix_rows, width)]
        pieces += [side.reshape(count, in_rows, width) for side in values]
    sizes = [piece.shape[1] for piece in pieces]
    back = lax.all_to_all(jnp.concatenate(pieces, 1), "seq", 0, 0, tiled=True)
    back = jnp.split(back, np.cumsum(sizes)[:-1].tolist(), axis=1)

    def columns(block):
        cut = block.reshape(count, -1, dp, share).transpose(1, 2, 0, 3)
        return cut.reshape(-1, gate_width).astype(F32)

    def value_share(sides):
        sides = jnp.stack(sides, 0)
        return sides.transpose(2, 0, 1, 3).reshape(in_rows, 2 * count * width).astype(F32)

    def out_share(block):
        return block.reshape(out_parts, mix_rows, width).transpose(1, 0, 2).reshape(mix_rows, model).astype(F32)

    gates, mixes, values = [], [], []
    for layer in range(depth):
        gate, mix, side_a, side_b = back[4 * layer : 4 * layer + 4]
        gates.append(columns(gate))
        mixes.append(columns(mix))
        values.append(value_share([side_a, side_b]))
    outs = [out_share(held[layer][3]) for layer in range(depth)]

    norm_all = jnp.stack(norm_grads).reshape(2 * depth, dp * count, in_rows).transpose(1, 0, 2)
    norm_all = norm_all.reshape(dp * count, 2 * depth * in_rows)
    norm_sum = jnp.sum(lax.all_to_all(norm_all, ("dp", "seq"), 0, 0, tiled=True), 0).reshape(depth, 2, in_rows)

    state_sum = ssm_sum[:, : 2 * depth * own].reshape(dp, depth, 2, own, both).transpose(1, 2, 0, 3, 4)
    coef_sum, rate_sum = state_sum[:, 0], state_sum[:, 1]
    skip_sum = ssm_sum[:, 2 * depth * own :].reshape(dp, 16, -1)[:, :depth, : 2 * own].transpose(1, 0, 2)
    return (
        stream,
        grad_stream,
        jnp.stack(gates),
        jnp.stack(values),
        jnp.stack(mixes),
        jnp.stack(outs),
        norm_sum[:, 0],
        norm_sum[:, 1],
        coef_sum.reshape(ssm_coef.shape),
        rate_sum.reshape(ssm_rate.shape),
        skip_sum.reshape(ssm_skip.shape),
    )


def solution(mesh):
    in_specs = (
        P(("dp", "seq"), None),
        P("dp"),
        P(("dp", "seq"), None),
        P(None, ("dp", "seq"), None),
        P(None, ("dp", "seq"), None),
        P(None, ("dp", "seq"), None),
        P(None, ("dp", "seq"), None),
        P(None, ("dp", "seq")),
        P(None, ("dp", "seq")),
        P(None, None, "seq", None),
        P(None, None, "seq", None),
        P(None, None, "seq"),
    )
    out_specs = (
        P(("dp", "seq"), None),
        P(("dp", "seq"), None),
        P(None, ("dp", "seq"), None),
        P(None, ("dp", "seq"), None),
        P(None, ("dp", "seq"), None),
        P(None, ("dp", "seq"), None),
        P(None, ("dp", "seq")),
        P(None, ("dp", "seq")),
        P(None, None, "seq", None),
        P(None, None, "seq", None),
        P(None, None, "seq"),
    )
    return jax.shard_map(shards, mesh=mesh, in_specs=in_specs, out_specs=out_specs, check_vma=False)
```

```python
from functools import partial

import numpy as np

import jax
import jax.numpy as jnp
from jax import lax
from jax.experimental import pallas as pl
from jax.experimental.layout import Layout, with_layout_constraint
from jax.experimental.pallas import tpu as pltpu
from jax.sharding import PartitionSpec as P

EPSILON = 1e-05
BF = jnp.bfloat16
F32 = jnp.float32
LANES = 128


def dot(left, right, left_dim, right_dim):
    return lax.dot_general(
        left, right, (((left_dim,), (right_dim,)), ((), ())), preferred_element_type=F32
    )


def wave_table(length):
    step = np.arange(length, dtype=np.int64)
    phase = ((2 * step[:, None] + 1) * step[None, :]) % (4 * length)
    angle = phase * (np.pi / (2 * length))
    return np.concatenate([np.cos(angle), np.sin(angle)], 0).astype(jnp.bfloat16)


def decay_tiles(rate):
    rows = lax.broadcasted_iota(jnp.int32, (8, LANES), 0).astype(F32)
    tiles = [jnp.exp(-rate * rows)]
    step = jnp.exp(-8.0 * jnp.broadcast_to(rate, (8, LANES)))
    while len(tiles) < LANES // 8:
        tiles = tiles + [tile * step for tile in tiles]
        step = step * step
    return tiles


def block_decays(rate, count):
    starts = lax.broadcasted_iota(jnp.int32, (count, LANES), 0).astype(F32) * float(LANES)
    return starts, jnp.exp(-rate * starts)


def spectra_kernel(unroll, rate_ref, coef_ref, sign_ref, wave_home, *refs):
    cos_ref, sin_ref, kern_ref, flat_ref, wave_ref, sem = refs[-6:]
    pairs = rate_ref.shape[0]
    length = wave_ref.shape[1]
    load = pltpu.make_async_copy(wave_home, wave_ref, sem)
    load.start()
    count = length // LANES
    lower = lax.broadcasted_iota(jnp.int32, (count, LANES), 1) < LANES // 2

    def pair(step, carry):
        for offset in range(unroll):
            index = step * unroll + offset
            rate = rate_ref[pl.ds(index, 1), :]
            near = jnp.concatenate(decay_tiles(rate), 0).astype(BF)
            far = block_decays(rate, count)[1] * (coef_ref[pl.ds(index, 1), :] * rate)
            left = jnp.concatenate([jnp.where(lower, far, 0.0), jnp.where(lower, 0.0, far)], 0)
            place = pl.ds(pl.multiple_of(index * 2 * count, 2 * count), 2 * count)
            kern_ref[place, :] = dot(left.astype(BF), near, 1, 1)
        return carry

    lax.fori_loop(0, pairs // unroll, pair, 0)
    for part in range(count):
        flat_ref[:, part * LANES : (part + 1) * LANES] = kern_ref[
            pl.ds(part, 2 * pairs, stride=count), :
        ].astype(BF)
    load.wait()
    chunk = 256
    for part in range(length // chunk):
        rows = slice(part * chunk, (part + 1) * chunk)
        cos_ref[rows, :] = dot(wave_ref[rows, :], flat_ref[...], 1, 1).astype(BF)
        sines = dot(wave_ref[length + part * chunk : length + (part + 1) * chunk, :], flat_ref[...], 1, 1)
        sin_ref[rows, :] = (sines * sign_ref[...]).astype(BF)


def channel_block(channels):
    return 256 if channels % 256 == 0 else channels


def unroll_of(pairs):
    return 16 if pairs % 16 == 0 else 8


def table_bytes(wave):
    return 2 * wave.shape[0] * wave.shape[1] + 12 * 2**20


def whole_table(wave):
    return pl.BlockSpec(wave.shape, lambda j: (0, 0), pipeline_mode=pl.Buffered(1))


def spectra(coef, rate, sign, wave, layer, part, earlier):
    channels = 2 * coef.shape[1]
    length = wave.shape[1]
    block = channel_block(channels)
    rows = pl.BlockSpec((None, block // 2, LANES), lambda j: (layer, part, 0))
    lanes = pl.BlockSpec((length, block), lambda j: (0, part))
    shape = jax.ShapeDtypeStruct((length, channels), BF)
    return pl.pallas_call(
        partial(spectra_kernel, unroll_of(block // 2)),
        out_shape=(shape, shape),
        grid=(1,),
        in_specs=[
            rows,
            rows,
            pl.BlockSpec((1, block), lambda j: (0, part)),
            pl.BlockSpec(memory_space=pltpu.HBM),
        ]
        + [pl.BlockSpec(memory_space=pl.ANY)] * len(earlier),
        out_specs=(lanes, lanes),
        scratch_shapes=[
            pltpu.VMEM((block * length // LANES, LANES), F32),
            pltpu.VMEM((block, length), BF),
            pltpu.VMEM(wave.shape, BF),
            pltpu.SemaphoreType.DMA,
        ],
        input_output_aliases={4 + j: j for j in range(len(earlier))},
        compiler_params=pltpu.CompilerParams(vmem_limit_bytes=table_bytes(wave)),
        cost_estimate=pl.CostEstimate(
            flops=12 * length * length * block,
            bytes_accessed=4 * length * length + 4 * length * block,
            transcendentals=0,
        ),
        name="spectra",
    )(rate, coef, sign, wave, *earlier)


def state_grads_kernel(
    unroll, rate_ref, coef_ref, cos_ref, sin_ref, wave_ref, coef_out, rate_out, turned_ref, kern_ref
):
    pairs = rate_ref.shape[0]
    length = wave_ref.shape[1]
    count = length // LANES
    lower = lax.broadcasted_iota(jnp.int32, (count, LANES), 1) < LANES // 2
    row = lax.broadcasted_iota(jnp.int32, (8, LANES), 0).astype(F32)
    turned_ref[:, :length] = cos_ref[...].T
    turned_ref[:, length:] = sin_ref[...].T
    chunk = 256
    for part in range(length // chunk):
        got = dot(turned_ref[...], wave_ref[:, part * chunk : (part + 1) * chunk], 1, 0)
        for side in range(chunk // LANES):
            place = pl.ds(part * (chunk // LANES) + side, 2 * pairs, stride=count)
            kern_ref[place, :] = got[:, side * LANES : (side + 1) * LANES]

    def pair(step, carry):
        for offset in range(unroll):
            index = step * unroll + offset
            rate = rate_ref[pl.ds(index, 1), :]
            coef = coef_ref[pl.ds(index, 1), :]
            tiles = decay_tiles(rate)
            near = jnp.concatenate(tiles, 0).astype(BF)
            lagged = jnp.concatenate([tile * (row + 8.0 * j) for j, tile in enumerate(tiles)], 0)
            place = pl.ds(pl.multiple_of(index * 2 * count, 2 * count), 2 * count)
            both = jnp.concatenate([near, lagged.astype(BF)], 1)
            got = dot(kern_ref[place, :].astype(BF), both, 1, 0)
            plain = jnp.where(lower, got[:count, :LANES], got[count:, :LANES])
            first = jnp.where(lower, got[:count, LANES:], got[count:, LANES:])
            starts, far = block_decays(rate, count)
            total = jnp.sum(far * plain, axis=0, keepdims=True)
            moment = jnp.sum(far * (starts * plain + first), axis=0, keepdims=True)
            coef_out[pl.ds(index, 1), :] = rate * total * (1.0 / length)
            rate_out[pl.ds(index, 1), :] = coef * (total - rate * moment) * (1.0 / length)
        return carry

    lax.fori_loop(0, pairs // unroll, pair, 0)


def state_grads(coef, rate, cosines, sines, wave, layer):
    channels = 2 * coef.shape[1]
    length = wave.shape[1]
    block = channel_block(channels)
    rows = pl.BlockSpec((None, block // 2, LANES), lambda j: (layer, j, 0))
    made = pl.BlockSpec((block // 2, LANES), lambda j: (j, 0))
    lanes = pl.BlockSpec((length, block), lambda j: (0, j))
    shape = jax.ShapeDtypeStruct(coef.shape[1:], F32)
    return pl.pallas_call(
        partial(state_grads_kernel, unroll_of(block // 2)),
        out_shape=(shape, shape),
        grid=(channels // block,),
        in_specs=[rows, rows, lanes, lanes, whole_table(wave)],
        out_specs=(made, made),
        scratch_shapes=[
            pltpu.VMEM((block, 2 * length), BF),
            pltpu.VMEM((block * length // LANES, LANES), F32),
        ],
        compiler_params=pltpu.CompilerParams(vmem_limit_bytes=table_bytes(wave)),
        cost_estimate=pl.CostEstimate(
            flops=12 * length * length * channels,
            bytes_accessed=4 * length * length + 4 * length * channels,
            transcendentals=0,
        ),
        name="state_grads",
    )(rate, coef, cosines, sines, wave)


def pairs_of(count, bit):
    return [(i, i ^ bit) for i in range(count)]


def seq_gather(block, count, wait):
    blocks = {0: block}
    bit = count // 2
    while bit:
        for member in list(blocks):
            blocks[member ^ bit] = lax.ppermute(blocks[member], "seq", pairs_of(count, bit))
        if bit == count // 2:
            blocks[bit], wait = together(blocks[bit], wait)
        bit //= 2
    return [blocks[m] for m in range(count)], wait


def seq_rows(block, count, wait):
    whole, wait = gather_bits(block, "seq", count, far_first(count), wait)
    return row_major(whole.reshape(count * block.shape[0], block.shape[1])), wait


def seq_reduce_rows(whole, count):
    blocks = whole.reshape(count, -1, whole.shape[1])
    return reduce_bits(blocks, "seq", count, bits_of(count), F32)


def row_major(array):
    return with_layout_constraint(array, Layout(tuple(range(array.ndim))))


def bits_of(count):
    return [1 << j for j in range(count.bit_length() - 1)]


def far_first(count):
    return bits_of(count)[::-1]


def y_first(count):
    return bits_of(count)


def z_first(count):
    return bits_of(count)[1:] + bits_of(count)[:1]


def swap(block, axis, count, bit):
    return lax.ppermute(block, axis, pairs_of(count, bit))


def join(block, other, axis, bit, done):
    upper = (lax.axis_index(axis) & bit) != 0
    pair = [jnp.where(upper, other, block), jnp.where(upper, block, other)]
    return jnp.stack(pair, done.index(bit))


def gather_bits(block, axis, count, sequence, wait=()):
    done = []
    for bit in sequence:
        other = swap(block, axis, count, bit)
        if not done:
            other, wait = together(other, wait)
        done = sorted(done + [bit], reverse=True)
        block = join(block, other, axis, bit, done)
    return block.reshape((count,) + block.shape[len(done) :]), wait


def cut_half(blocks, axis, count, bit, turn=0):
    level = far_first(count).index(bit)
    side = ((lax.axis_index(axis) ^ turn) // bit) % 2
    sent = lax.dynamic_slice_in_dim(blocks, 1 - side, 1, level).astype(BF)
    return lax.dynamic_slice_in_dim(blocks, side, 1, level), sent


def add_half(held, came, kind):
    return (held.astype(F32) + came.astype(F32)).astype(kind)


def bit_blocks(blocks, count):
    return blocks.reshape((2,) * len(bits_of(count)) + blocks.shape[1:])


def reduce_bits(blocks, axis, count, sequence, kind):
    blocks = bit_blocks(blocks, count)
    for bit in sequence:
        held, sent = cut_half(blocks, axis, count, bit)
        blocks = add_half(held, swap(sent, axis, count, bit), kind)
    return blocks.reshape(blocks.shape[len(bits_of(count)) :])


def together(*arrays):
    return lax.optimization_barrier(arrays)


def gelu_parts(pre):
    share = 0.5 * (1.0 + lax.erf(pre * np.float32(np.sqrt(0.5))))
    slope = share + pre * (jnp.exp(-0.5 * pre * pre) * np.float32(1.0 / np.sqrt(2.0 * np.pi)))
    return pre * share, slope


def normalize(stream):
    centre = jnp.mean(stream, axis=-1, keepdims=True)
    centred = stream - centre
    spread = jnp.mean(centred * centred, axis=-1, keepdims=True)
    factor = lax.rsqrt(spread + EPSILON)
    return centred * factor, factor


def turned(spectrum):
    return jnp.stack([-spectrum[1], spectrum[0]])


def run_layer(stream, rows_all, keep, norm, early, late, hat, skip, tables, count, beside_rows, beside_product):
    gain, bias = norm
    waves, waves_back = tables
    length = waves.shape[1]
    xhat, factor = normalize(stream)
    if rows_all is None:
        own, wait = beside_rows((xhat * gain + bias).astype(BF))
        normed, wait = seq_rows(own, count, wait)
    else:
        normed, wait = (normalize(rows_all.astype(F32))[0] * gain + bias).astype(BF), ()
    w_value = early(wait)
    value_act, value_slope = gelu_parts(dot(normed, w_value, 1, 0))
    values = (value_act * keep).astype(BF)
    value_slope = (value_slope * keep).astype(BF)
    values, value_slope = together(values, value_slope)
    x_hat = dot(waves, values, 1, 0).astype(BF)
    k_cos, k_sin = hat()
    x_cos, x_sin = x_hat[:length].astype(F32), x_hat[length:].astype(F32)
    y_hat = jnp.concatenate([k_cos * x_cos - k_sin * x_sin, k_cos * x_sin + k_sin * x_cos], 0).astype(BF)
    mixes = dot(waves_back, y_hat, 1, 0) * (1.0 / length) + skip * values.astype(F32)
    width = mixes.shape[1] // 2
    product = (mixes[:, :width] * mixes[:, width:]).astype(BF)
    product, mixes = together(product, mixes.astype(BF))
    product, wait = beside_product(product)
    products, wait = seq_gather(product, count, wait)
    w_gate, w_mix, w_out = late(wait)
    gate_act, gate_slope = gelu_parts(dot(normed, w_gate, 1, 0))
    update = dot(products[0], w_mix[0], 1, 0)
    for member in range(1, count):
        update = update + dot(products[member], w_mix[member], 1, 0)
    mixed = (update * gate_act).astype(BF)
    gate_back = (update * gate_slope).astype(BF)
    mixed, gate_act, gate_back = together(mixed, gate_act.astype(BF), gate_back)
    result = stream + seq_reduce_rows(dot(mixed, w_out, 1, 0), count)
    saved = (
        xhat,
        factor,
        normed,
        gate_act,
        gate_back,
        value_slope,
        values,
        x_hat,
        mixes,
        products,
        mixed,
    )
    return result, saved


def back_gate(grad_stream, saved, late, count, wait):
    w_gate, w_mix, w_out = late
    xhat, factor, normed, gate_act, gate_back, value_slope, values, x_hat, mixes, products, mixed = saved
    out_low, wait = seq_rows(grad_stream, count, wait)
    grad_mixed = dot(out_low, w_out, 1, 1)
    update_low = (grad_mixed * gate_act.astype(F32)).astype(BF)
    gate_grad = (grad_mixed * gate_back.astype(F32)).astype(BF)
    update_low, gate_grad = together(update_low, gate_grad)
    width = products[0].shape[1]
    model = out_low.shape[1]
    blocks = dict(enumerate(dot(update_low, w_mix[m], 1, 1) for m in range(count)))
    for bit in bits_of(count):
        for member in sorted(blocks, reverse=True):
            if member & bit:
                sent = blocks.pop(member).astype(BF)
                if member == count // 2:
                    sent, update_low, gate_grad, out_low = together(sent, update_low, gate_grad, out_low)
                blocks[member ^ bit] = add_half(blocks[member ^ bit], swap(sent, "seq", count, bit), F32)
    product_low = blocks[0]
    grad_out = [
        dot(mixed, out_low[:, j * width : (j + 1) * width], 0, 0).astype(BF) for j in range(model // width)
    ]
    grad_mix = [dot(products[m], update_low, 0, 0).astype(BF) for m in range(count)]
    grad_gate = dot(normed, gate_grad, 0, 0).astype(BF)
    gate_part = dot(gate_grad, w_gate, 1, 1)
    return product_low.astype(BF), gate_part, (grad_gate, grad_mix, grad_out), wait


def back_convolution(product_low, saved, hat, skip, tables):
    xhat, factor, normed, gate_act, gate_back, value_slope, values, x_hat, mixes, products, mixed = saved
    waves, waves_back = tables
    length = waves.shape[1]
    width = product_low.shape[1]
    product_low = product_low.astype(F32)
    mixes = mixes.astype(F32)
    back = jnp.concatenate([product_low * mixes[:, width:], product_low * mixes[:, :width]], 1).astype(BF)
    g_hat = dot(waves, back, 1, 0).astype(BF)
    k_cos, k_sin = hat
    g_cos, g_sin = g_hat[:length].astype(F32), g_hat[length:].astype(F32)
    y_hat = jnp.concatenate([k_cos * g_cos + k_sin * g_sin, k_cos * g_sin - k_sin * g_cos], 0).astype(BF)
    grad_values = dot(waves_back, y_hat, 1, 0) * (1.0 / length) + skip * back.astype(F32)
    x_cos, x_sin = x_hat[:length].astype(F32), x_hat[length:].astype(F32)
    sign = jnp.concatenate([jnp.ones((width,), F32), -jnp.ones((width,), F32)])
    kern_hat = (
        (g_cos * x_cos + g_sin * x_sin).astype(BF),
        ((g_sin * x_cos - g_cos * x_sin) * sign).astype(BF),
    )
    grad_skip = jnp.sum(back.astype(F32) * values.astype(F32), axis=0)
    value_grad = (grad_values.astype(BF).astype(F32) * value_slope.astype(F32)).astype(BF)
    return value_grad, kern_hat, grad_skip


def back_norm(grad_stream, grad_normed, saved, gain):
    xhat, factor = saved[:2]
    norm_terms = jnp.stack([jnp.sum(grad_normed * xhat, 0), jnp.sum(grad_normed, 0)])
    inner = grad_normed * gain
    slope = jnp.mean(inner, axis=-1, keepdims=True)
    tilt = jnp.mean(inner * xhat, axis=-1, keepdims=True)
    return grad_stream + (inner - slope - xhat * tilt) * factor, norm_terms


def shards(tokens, lengths, cotangent, w_gate, w_value, w_mix, w_out, ln_gain, ln_bias, ssm_coef, ssm_rate, ssm_skip):
    dp = lax.axis_size("dp")
    count = lax.axis_size("seq")
    rows, model = tokens.shape
    length = rows * count
    depth, in_rows, gate_width = w_gate.shape
    mix_rows = w_mix.shape[1]
    width = ssm_coef.shape[2]
    states = ssm_coef.shape[3]
    share = gate_width // (dp * count)
    out_parts = model // width
    order = [lax.axis_index("seq") ^ m for m in range(count)]
    keep = (jnp.arange(length, dtype=jnp.int32) < lengths[0]).astype(F32)[:, None]
    table = wave_table(length)
    waves = jnp.asarray(table)
    tables = (waves, jnp.asarray(np.ascontiguousarray(table.T)))

    def by_column(weight):
        cut = weight.reshape(weight.shape[0], dp, count, share)
        return cut.transpose(2, 0, 1, 3).reshape(count, weight.shape[0], width)

    def value_columns(layer):
        cut = w_value[layer].reshape(in_rows, 2, count, width).transpose(2, 1, 0, 3)
        return cut.reshape(count, 2 * in_rows, width)

    norm_rows = jnp.stack([ln_gain, ln_bias], 1).reshape(2 * depth, in_rows)
    norm_rows = jnp.pad(norm_rows, ((0, 16 - 2 * depth), (0, width - in_rows)))
    first = jnp.concatenate([value_columns(0), jnp.broadcast_to(norm_rows, (count,) + norm_rows.shape)], 1)
    first, tokens = together(first, tokens)
    first = lax.all_to_all(first, "seq", 0, 0, tiled=True)
    rows_all, _ = seq_rows(tokens, count, ())
    pieces = [by_column(w_gate[0]), by_column(w_mix[0])]
    for layer in range(1, depth):
        pieces += [value_columns(layer), by_column(w_gate[layer]), by_column(w_mix[layer])]
    sizes = [piece.shape[1] for piece in pieces]
    first, rest = together(first, jnp.concatenate(pieces, 1))

    coefs = ssm_coef.reshape(depth, width, 2 * states)
    rates = ssm_rate.reshape(depth, width, 2 * states)
    skips = ssm_skip.reshape(depth, 2 * width)
    sign = jnp.concatenate([jnp.ones((1, width), F32), -jnp.ones((1, width), F32)], 1)
    table_parts = 2 * width // channel_block(2 * width)

    def make_tables(layer, parts_made, hat, tie):
        rate, tie = together(rates, tie)
        for part in parts_made:
            hat = spectra(coefs, rate, sign, waves, layer, part, hat)
        return hat, tie

    def flat(piece):
        return piece.reshape(-1, width)

    def value_sides(piece):
        return [flat(piece[:, side * in_rows : (side + 1) * in_rows]) for side in range(2)]

    def out_sides(layer):
        return [w_out[layer][:, j * width : (j + 1) * width] for j in range(out_parts)]

    norm_piece = first[:, 2 * in_rows :, :in_rows].transpose(1, 0, 2).reshape(16, count * in_rows)
    norm_piece = jnp.pad(norm_piece, ((0, 0), (0, -(count * in_rows) % width)))
    sides = value_sides(first)
    n_in = count * in_rows
    pair = [jnp.concatenate([sides[0], flat(norm_piece)], 0), sides[1]]
    paths = [far_first(dp), y_first(dp)[:1] + far_first(dp)[:-1]]
    pair, rest = together(pair, rest)
    rest = lax.all_to_all(rest, "seq", 0, 0, tiled=True)
    rest = jnp.split(rest, np.cumsum(sizes)[:-1].tolist(), axis=1)
    late_block = jnp.concatenate([flat(rest[0]), flat(rest[1])] + out_sides(0), 0)
    done = [[], []]
    hat = ()
    for step in range(len(bits_of(dp))):
        others = [swap(block, "dp", dp, path[step]) for block, path in zip(pair, paths)]
        if step < table_parts:
            hat, pair = make_tables(0, [step], hat, pair)
            others, hat = together(others, hat)
        if step == 1:
            others, late_block = together(others, late_block)
        for j in range(2):
            done[j] = sorted(done[j] + [paths[j][step]], reverse=True)
            pair[j] = join(pair[j], others[j], "dp", paths[j][step], done[j])
    hat, pair = make_tables(0, range(len(bits_of(dp)), table_parts), hat, pair)
    hats = [hat]
    pair, rows_all = together(pair, rows_all)
    side_a, side_b = [block.reshape((dp,) + block.shape[-2:]) for block in pair]
    norms = side_a[:, n_in:].reshape(dp, 16, -1)[:, : 2 * depth, :n_in]
    norms = norms.transpose(1, 0, 2).reshape(depth, 2, model).astype(F32)

    def value_weight(side_a, side_b):
        return jnp.concatenate([side_a.reshape(model, width), side_b.reshape(model, width)], 1)

    def mix_weight(block):
        block = block.reshape(count, width, width)
        return [lax.dynamic_index_in_dim(block, order[m], 0, keepdims=False) for m in range(count)]

    def out_weight(block):
        cut = block.reshape(dp, out_parts, mix_rows, width).transpose(0, 2, 1, 3)
        return cut.reshape(dp * mix_rows, model)

    early = [(value_weight(side_a[:, :n_in], side_b), norms[0, 0], norms[0, 1])]
    got_late = lax.all_gather(late_block, "dp", axis=0)

    def late_weights(got):
        gate, mix, out = jnp.split(got, [n_in, n_in + count * mix_rows], axis=1)
        return gate.reshape(model, width), mix_weight(mix), out_weight(out)

    def layer_block(layer):
        value, gate, mix = rest[3 * layer - 1 : 3 * layer + 2]
        return jnp.concatenate(value_sides(value) + [flat(gate), flat(mix)] + out_sides(layer), 0)

    got_layers = [None] + [lax.all_gather(layer_block(layer), "dp", axis=0) for layer in range(1, depth)]

    late = []
    stream = tokens.astype(F32)
    kept = []
    for layer in range(depth):

        def beside_rows(own):
            return own, got_layers[layer]

        def early_weights(got):
            if layer:
                side_a, side_b, got = jnp.split(got, [n_in, 2 * n_in], axis=1)
                early.append((value_weight(side_a, side_b), norms[layer, 0], norms[layer, 1]))
                late.append(late_weights(got))
            return early[layer][0]

        def beside_product(product):
            hat = ()
            if layer + 1 < depth:
                hat, product = make_tables(layer + 1, range(table_parts), (), product)
            return product, (() if layer else got_late, hat)

        def later_weights(wait):
            if not layer:
                late.append(late_weights(wait[0]))
            hats.append(wait[1])
            return late[layer]

        stream, saved = run_layer(
            stream, None if layer else rows_all, keep, norms[layer], early_weights, later_weights,
            lambda: hats[layer], skips[layer], tables, count, beside_rows, beside_product,
        )
        kept.append(saved)

    def owner_pieces(rows_list):
        pieces = [piece.reshape(count, -1, width) for piece in rows_list]
        return jnp.concatenate(pieces, 1), np.cumsum([piece.shape[1] for piece in pieces])[:-1].tolist()

    def natural(blocks):
        whole = jnp.zeros((count,) + blocks[0].shape, blocks[0].dtype)
        for member, block in enumerate(blocks):
            whole = lax.dynamic_update_index_in_dim(whole, block, order[member], 0)
        return whole

    grad_stream = cotangent.astype(F32)
    norm_grads = [None] * depth
    ssm_grads = [None] * depth
    held = [None] * depth
    kern_hat = None
    turn = lax.axis_index("seq") * (dp // count)
    paths = [y_first(dp), z_first(dp), y_first(dp)]
    turns = [turn, 0, 0]

    def sent_dp(pairs, at):
        return [
            (pair[0], swap(pair[1], "dp", dp, path[step])) for pair, path, step in zip(pairs, paths, at)
        ]

    def next_dp(pairs, at):
        return [
            cut_half(add_half(*pair, BF), "dp", dp, path[step], side)
            for pair, path, side, step in zip(pairs, paths, turns, at)
        ]

    for layer in reversed(range(depth)):
        low = grad_stream.astype(BF)
        wait = ()
        if kern_hat is not None:
            low, kern_hat = together(low, kern_hat)
            wait = state_grads(coefs, rates, *kern_hat, waves, layer + 1)
        product_low, gate_part, terms, wait = back_gate(low, kept[layer], late[layer], count, wait)
        if kern_hat is not None:
            ssm_grads[layer + 1] += wait
        grad_gate, grad_mix, grad_out = terms
        others = [grad_gate.reshape(dp, n_in, width)] + [g.reshape(dp, mix_rows, width) for g in grad_out]
        if not layer:
            blocks = [jnp.stack(grad_mix).reshape(dp, count * mix_rows, width), jnp.concatenate(others, 1)]
            moving = [
                cut_half(bit_blocks(block, dp), "dp", dp, path[0], side)
                for block, path, side in zip(blocks, paths, turns)
            ]
            product_low, moving = together(product_low, moving)
            moving = sent_dp(moving, (0, 0))
        value_grad, kern_hat, grad_skip = back_convolution(product_low, kept[layer], hats[layer], skips[layer], tables)
        ssm_grads[layer] = (grad_skip,)
        if not layer:
            value_grad, moving = together(value_grad, moving)
            moving = next_dp(moving, (1, 1))
        normed = kept[layer][2]
        values = dot(normed, value_grad, 0, 0).astype(BF).reshape(dp, n_in, 2 * width)
        parts = dot(value_grad, early[layer][0], 1, 1) + gate_part
        sums = bit_blocks(parts.reshape(count, rows, model), count)
        if layer:
            block = [natural(grad_mix).reshape(dp, count * mix_rows, width)] + others
            block = jnp.concatenate(block + [values[:, :, :width], values[:, :, width:]], 1)
            held[layer] = lax.psum_scatter(block, "dp", scatter_dimension=0, tiled=False)
        else:
            moving.append(cut_half(bit_blocks(values, dp), "dp", dp, paths[2][0]))
        for step, bit in enumerate(bits_of(count)):
            held_rows, sent = cut_half(sums, "seq", count, bit)
            if step == 1 and not layer:
                sent, moving, kern_hat = together(sent, moving, kern_hat)
                came = swap(sent, "seq", count, bit)
                moving = sent_dp(moving, (1, 1, 0))
                last = state_grads(coefs, rates, *kern_hat, waves, 0)
                came, moving, last = together(came, moving, last)
                ssm_grads[0] += last
            else:
                came = swap(sent, "seq", count, bit)
            sums = add_half(held_rows, came, F32)
        grad_normed = sums.reshape(rows, model)
        grad_stream, norm_grads[layer] = back_norm(grad_stream, grad_normed, kept[layer], early[layer][1])

    own = width // dp
    both = 2 * states
    norm_all = jnp.stack(norm_grads).reshape(2 * depth, dp, n_in).transpose(1, 0, 2)
    lanes = -(-max(2 * own, n_in) // both) * both
    skip_rows = jnp.stack([g[0].reshape(dp, 2 * own) for g in ssm_grads], 1)
    skip_rows = jnp.concatenate(
        [
            jnp.pad(skip_rows, ((0, 0), (0, 0), (0, lanes - 2 * own))),
            jnp.pad(norm_all, ((0, 0), (0, 16 - 3 * depth), (0, lanes - n_in))),
        ],
        1,
    ).reshape(dp, -1, both)
    states_all = jnp.stack([g[j].reshape(dp, own, both) for g in ssm_grads for j in (1, 2)], 1).astype(BF)
    ssm_rows = jnp.concatenate([states_all.reshape(dp, 2 * depth * own, both), skip_rows.astype(BF)], 1)

    sums = [add_half(*pair, BF) for pair in moving] + [bit_blocks(ssm_rows, dp)]
    paths = [paths[0][2:], paths[1][2:], paths[2][1:], y_first(dp)]
    turns = turns + [0]

    def flat_sum(j):
        return sums[j].reshape(sums[j].shape[-2:])

    first_round = True
    while any(paths):
        active = [j for j, path in enumerate(paths) if path]
        pairs = [cut_half(sums[j], "dp", dp, paths[j][0], turns[j]) for j in active]
        pairs = lax.optimization_barrier(pairs)
        pairs = [(pair[0], swap(pair[1], "dp", dp, paths[j][0])) for j, pair in zip(active, pairs)]
        if first_round:
            pairs, held = together(pairs, held)
            first_round = False
        else:
            pairs = lax.optimization_barrier(pairs)
        for j, pair in zip(active, pairs):
            sums[j] = add_half(*pair, BF)
            paths[j] = paths[j][1:]
    own_sum = flat_sum(3)
    norm_own = own_sum[2 * depth * own :].reshape(16, lanes)[depth : 3 * depth, :n_in]
    norm_own = norm_own.reshape(2 * depth, count, in_rows).transpose(1, 0, 2)
    norm_own = jnp.pad(norm_own, ((0, 0), (0, 16 - 2 * depth), (0, width - in_rows)))
    cuts = np.cumsum([count * mix_rows, n_in, out_parts * mix_rows, n_in]).tolist()
    value_sums = flat_sum(2)
    rows_list = [flat_sum(1)[:n_in], flat_sum(0), value_sums[:, :width], value_sums[:, width:]]
    outs = [flat_sum(1)[n_in:]]
    for layer in range(1, depth):
        mix, gate, out, side_a, side_b = jnp.split(held[layer], cuts, axis=0)
        outs.append(out)
        rows_list += [gate, mix, side_a, side_b]
    last, last_cuts = owner_pieces(rows_list + [norm_own.reshape(count * 16, width)])
    own_sum, last = together(own_sum, last)
    last = lax.all_to_all(last, "seq", 0, 0, tiled=True)
    ssm_sum, last = gather_bits(own_sum, "dp", dp, far_first(dp), last)
    ssm_sum = ssm_sum.astype(F32)
    back_parts = jnp.split(last, last_cuts, axis=1)
    norm_came = back_parts.pop()
    back = back_parts
    norm_sum = jnp.sum(norm_came[:, : 2 * depth, :in_rows].astype(F32), 0).reshape(depth, 2, in_rows)

    def columns(block):
        cut = block.reshape(count, -1, dp, share).transpose(1, 2, 0, 3)
        return cut.reshape(-1, gate_width).astype(F32)

    def value_share(sides):
        sides = jnp.stack(sides, 0)
        return sides.transpose(2, 0, 1, 3).reshape(in_rows, 2 * count * width).astype(F32)

    def out_share(block):
        return block.reshape(out_parts, mix_rows, width).transpose(1, 0, 2).reshape(mix_rows, model).astype(F32)

    gates, mixes, values = [], [], []
    for layer in range(depth):
        gate, mix, side_a, side_b = back[4 * layer : 4 * layer + 4]
        gates.append(columns(gate))
        mixes.append(columns(mix))
        values.append(value_share([side_a, side_b]))
    outs = [out_share(out) for out in outs]

    state_sum = ssm_sum[:, : 2 * depth * own].reshape(dp, depth, 2, own, both).transpose(1, 2, 0, 3, 4)
    coef_sum, rate_sum = state_sum[:, 0], state_sum[:, 1]
    skip_sum = ssm_sum[:, 2 * depth * own :].reshape(dp, 16, lanes)[:, :depth, : 2 * own].transpose(1, 0, 2)
    return (
        stream,
        grad_stream,
        jnp.stack(gates),
        jnp.stack(values),
        jnp.stack(mixes),
        jnp.stack(outs),
        norm_sum[:, 0],
        norm_sum[:, 1],
        coef_sum.reshape(ssm_coef.shape),
        rate_sum.reshape(ssm_rate.shape),
        skip_sum.reshape(ssm_skip.shape),
    )


def solution(mesh):
    in_specs = (
        P(("dp", "seq"), None),
        P("dp"),
        P(("dp", "seq"), None),
        P(None, ("dp", "seq"), None),
        P(None, ("dp", "seq"), None),
        P(None, ("dp", "seq"), None),
        P(None, ("dp", "seq"), None),
        P(None, ("dp", "seq")),
        P(None, ("dp", "seq")),
        P(None, None, "seq", None),
        P(None, None, "seq", None),
        P(None, None, "seq"),
    )
    out_specs = (
        P(("dp", "seq"), None),
        P(("dp", "seq"), None),
        P(None, ("dp", "seq"), None),
        P(None, ("dp", "seq"), None),
        P(None, ("dp", "seq"), None),
        P(None, ("dp", "seq"), None),
        P(None, ("dp", "seq")),
        P(None, ("dp", "seq")),
        P(None, None, "seq", None),
        P(None, None, "seq", None),
        P(None, None, "seq"),
    )
    return jax.shard_map(shards, mesh=mesh, in_specs=in_specs, out_specs=out_specs, check_vma=False)
```

```python
from functools import partial

import numpy as np

import jax
import jax.numpy as jnp
from jax import lax
from jax.experimental import pallas as pl
from jax.experimental.layout import Layout, with_layout_constraint
from jax.experimental.pallas import tpu as pltpu
from jax.sharding import PartitionSpec as P

EPSILON = 1e-05
BF = jnp.bfloat16
F32 = jnp.float32
LANES = 128


def dot(left, right, left_dim, right_dim):
    return lax.dot_general(
        left, right, (((left_dim,), (right_dim,)), ((), ())), preferred_element_type=F32
    )


def wave_table(length):
    step = np.arange(length, dtype=np.int64)
    phase = ((2 * step[:, None] + 1) * step[None, :]) % (4 * length)
    angle = phase * (np.pi / (2 * length))
    return np.concatenate([np.cos(angle), np.sin(angle)], 0).astype(jnp.bfloat16)


def decay_tiles(rate):
    rows = lax.broadcasted_iota(jnp.int32, (8, LANES), 0).astype(F32)
    tiles = [jnp.exp(-rate * rows)]
    step = jnp.exp(-8.0 * jnp.broadcast_to(rate, (8, LANES)))
    while len(tiles) < LANES // 8:
        tiles = tiles + [tile * step for tile in tiles]
        step = step * step
    return tiles


def block_decays(rate, count):
    starts = lax.broadcasted_iota(jnp.int32, (count, LANES), 0).astype(F32) * float(LANES)
    return starts, jnp.exp(-rate * starts)


def spectra_kernel(unroll, rate_ref, coef_ref, sign_ref, wave_home, *refs):
    cos_ref, sin_ref, kern_ref, flat_ref, wave_ref, sem = refs[-6:]
    pairs = rate_ref.shape[0]
    length = wave_ref.shape[1]
    load = pltpu.make_async_copy(wave_home, wave_ref, sem)
    load.start()
    count = length // LANES
    lower = lax.broadcasted_iota(jnp.int32, (count, LANES), 1) < LANES // 2

    def pair(step, carry):
        for offset in range(unroll):
            index = step * unroll + offset
            rate = rate_ref[pl.ds(index, 1), :]
            near = jnp.concatenate(decay_tiles(rate), 0).astype(BF)
            far = block_decays(rate, count)[1] * (coef_ref[pl.ds(index, 1), :] * rate)
            left = jnp.concatenate([jnp.where(lower, far, 0.0), jnp.where(lower, 0.0, far)], 0)
            place = pl.ds(pl.multiple_of(index * 2 * count, 2 * count), 2 * count)
            kern_ref[place, :] = dot(left.astype(BF), near, 1, 1)
        return carry

    lax.fori_loop(0, pairs // unroll, pair, 0)
    for part in range(count):
        flat_ref[:, part * LANES : (part + 1) * LANES] = kern_ref[
            pl.ds(part, 2 * pairs, stride=count), :
        ].astype(BF)
    load.wait()
    chunk = 256
    for part in range(length // chunk):
        rows = slice(part * chunk, (part + 1) * chunk)
        cos_ref[rows, :] = dot(wave_ref[rows, :], flat_ref[...], 1, 1).astype(BF)
        sines = dot(wave_ref[length + part * chunk : length + (part + 1) * chunk, :], flat_ref[...], 1, 1)
        sin_ref[rows, :] = (sines * sign_ref[...]).astype(BF)


def channel_block(channels):
    return 256 if channels % 256 == 0 else channels


def unroll_of(pairs):
    return 16 if pairs % 16 == 0 else 8


def table_bytes(wave):
    return 2 * wave.shape[0] * wave.shape[1] + 12 * 2**20


def whole_table(wave):
    return pl.BlockSpec(wave.shape, lambda j: (0, 0), pipeline_mode=pl.Buffered(1))


def spectra(coef, rate, sign, wave, layer, part, earlier):
    channels = 2 * coef.shape[1]
    length = wave.shape[1]
    block = channel_block(channels)
    rows = pl.BlockSpec((None, block // 2, LANES), lambda j: (layer, part, 0))
    lanes = pl.BlockSpec((length, block), lambda j: (0, part))
    shape = jax.ShapeDtypeStruct((length, channels), BF)
    return pl.pallas_call(
        partial(spectra_kernel, unroll_of(block // 2)),
        out_shape=(shape, shape),
        grid=(1,),
        in_specs=[
            rows,
            rows,
            pl.BlockSpec((1, block), lambda j: (0, part)),
            pl.BlockSpec(memory_space=pltpu.HBM),
        ]
        + [pl.BlockSpec(memory_space=pl.ANY)] * len(earlier),
        out_specs=(lanes, lanes),
        scratch_shapes=[
            pltpu.VMEM((block * length // LANES, LANES), F32),
            pltpu.VMEM((block, length), BF),
            pltpu.VMEM(wave.shape, BF),
            pltpu.SemaphoreType.DMA,
        ],
        input_output_aliases={4 + j: j for j in range(len(earlier))},
        compiler_params=pltpu.CompilerParams(vmem_limit_bytes=table_bytes(wave)),
        cost_estimate=pl.CostEstimate(
            flops=12 * length * length * block,
            bytes_accessed=4 * length * length + 4 * length * block,
            transcendentals=0,
        ),
        name="spectra",
    )(rate, coef, sign, wave, *earlier)


def state_grads_kernel(
    unroll, rate_ref, coef_ref, cos_ref, sin_ref, wave_ref, coef_out, rate_out, turned_ref, kern_ref
):
    pairs = rate_ref.shape[0]
    length = wave_ref.shape[1]
    count = length // LANES
    lower = lax.broadcasted_iota(jnp.int32, (count, LANES), 1) < LANES // 2
    row = lax.broadcasted_iota(jnp.int32, (8, LANES), 0).astype(F32)
    turned_ref[:, :length] = cos_ref[...].T
    turned_ref[:, length:] = sin_ref[...].T
    chunk = 256
    for part in range(length // chunk):
        got = dot(turned_ref[...], wave_ref[:, part * chunk : (part + 1) * chunk], 1, 0)
        for side in range(chunk // LANES):
            place = pl.ds(part * (chunk // LANES) + side, 2 * pairs, stride=count)
            kern_ref[place, :] = got[:, side * LANES : (side + 1) * LANES]

    def pair(step, carry):
        for offset in range(unroll):
            index = step * unroll + offset
            rate = rate_ref[pl.ds(index, 1), :]
            coef = coef_ref[pl.ds(index, 1), :]
            tiles = decay_tiles(rate)
            near = jnp.concatenate(tiles, 0).astype(BF)
            lagged = jnp.concatenate([tile * (row + 8.0 * j) for j, tile in enumerate(tiles)], 0)
            place = pl.ds(pl.multiple_of(index * 2 * count, 2 * count), 2 * count)
            both = jnp.concatenate([near, lagged.astype(BF)], 1)
            got = dot(kern_ref[place, :].astype(BF), both, 1, 0)
            plain = jnp.where(lower, got[:count, :LANES], got[count:, :LANES])
            first = jnp.where(lower, got[:count, LANES:], got[count:, LANES:])
            starts, far = block_decays(rate, count)
            total = jnp.sum(far * plain, axis=0, keepdims=True)
            moment = jnp.sum(far * (starts * plain + first), axis=0, keepdims=True)
            coef_out[pl.ds(index, 1), :] = rate * total * (1.0 / length)
            rate_out[pl.ds(index, 1), :] = coef * (total - rate * moment) * (1.0 / length)
        return carry

    lax.fori_loop(0, pairs // unroll, pair, 0)


def state_grads(coef, rate, cosines, sines, wave, layer):
    channels = 2 * coef.shape[1]
    length = wave.shape[1]
    block = channel_block(channels)
    rows = pl.BlockSpec((None, block // 2, LANES), lambda j: (layer, j, 0))
    made = pl.BlockSpec((block // 2, LANES), lambda j: (j, 0))
    lanes = pl.BlockSpec((length, block), lambda j: (0, j))
    shape = jax.ShapeDtypeStruct(coef.shape[1:], F32)
    return pl.pallas_call(
        partial(state_grads_kernel, unroll_of(block // 2)),
        out_shape=(shape, shape),
        grid=(channels // block,),
        in_specs=[rows, rows, lanes, lanes, whole_table(wave)],
        out_specs=(made, made),
        scratch_shapes=[
            pltpu.VMEM((block, 2 * length), BF),
            pltpu.VMEM((block * length // LANES, LANES), F32),
        ],
        compiler_params=pltpu.CompilerParams(vmem_limit_bytes=table_bytes(wave)),
        cost_estimate=pl.CostEstimate(
            flops=12 * length * length * channels,
            bytes_accessed=4 * length * length + 4 * length * channels,
            transcendentals=0,
        ),
        name="state_grads",
    )(rate, coef, cosines, sines, wave)


def pairs_of(count, bit):
    return [(i, i ^ bit) for i in range(count)]


def seq_gather(block, count, wait):
    blocks = {0: block}
    bit = count // 2
    while bit:
        for member in list(blocks):
            blocks[member ^ bit] = lax.ppermute(blocks[member], "seq", pairs_of(count, bit))
        if bit == count // 2:
            blocks[bit], wait = together(blocks[bit], wait)
        bit //= 2
    return [blocks[m] for m in range(count)], wait


def seq_rows(block, count, wait):
    whole, wait = gather_bits(block, "seq", count, far_first(count), wait)
    return row_major(whole.reshape(count * block.shape[0], block.shape[1])), wait


def seq_reduce_rows(whole, count):
    blocks = whole.reshape(count, -1, whole.shape[1])
    return reduce_bits(blocks, "seq", count, bits_of(count), F32)


def row_major(array):
    return with_layout_constraint(array, Layout(tuple(range(array.ndim))))


def bits_of(count):
    return [1 << j for j in range(count.bit_length() - 1)]


def far_first(count):
    return bits_of(count)[::-1]


def y_first(count):
    return bits_of(count)


def z_first(count):
    return bits_of(count)[1:] + bits_of(count)[:1]


def swap(block, axis, count, bit):
    return lax.ppermute(block, axis, pairs_of(count, bit))


def join(block, other, axis, bit, done):
    upper = (lax.axis_index(axis) & bit) != 0
    pair = [jnp.where(upper, other, block), jnp.where(upper, block, other)]
    return jnp.stack(pair, done.index(bit))


def gather_bits(block, axis, count, sequence, wait=()):
    done = []
    for bit in sequence:
        other = swap(block, axis, count, bit)
        if not done:
            other, wait = together(other, wait)
        done = sorted(done + [bit], reverse=True)
        block = join(block, other, axis, bit, done)
    return block.reshape((count,) + block.shape[len(done) :]), wait


def cut_half(blocks, axis, count, bit, turn=0):
    level = far_first(count).index(bit)
    side = ((lax.axis_index(axis) ^ turn) // bit) % 2
    sent = lax.dynamic_slice_in_dim(blocks, 1 - side, 1, level).astype(BF)
    return lax.dynamic_slice_in_dim(blocks, side, 1, level), sent


def add_half(held, came, kind):
    return (held.astype(F32) + came.astype(F32)).astype(kind)


def bit_blocks(blocks, count):
    return blocks.reshape((2,) * len(bits_of(count)) + blocks.shape[1:])


def reduce_bits(blocks, axis, count, sequence, kind):
    blocks = bit_blocks(blocks, count)
    for bit in sequence:
        held, sent = cut_half(blocks, axis, count, bit)
        blocks = add_half(held, swap(sent, axis, count, bit), kind)
    return blocks.reshape(blocks.shape[len(bits_of(count)) :])


def together(*arrays):
    return lax.optimization_barrier(arrays)


def gelu_parts(pre):
    share = 0.5 * (1.0 + lax.erf(pre * np.float32(np.sqrt(0.5))))
    slope = share + pre * (jnp.exp(-0.5 * pre * pre) * np.float32(1.0 / np.sqrt(2.0 * np.pi)))
    return pre * share, slope


def normalize(stream):
    centre = jnp.mean(stream, axis=-1, keepdims=True)
    centred = stream - centre
    spread = jnp.mean(centred * centred, axis=-1, keepdims=True)
    factor = lax.rsqrt(spread + EPSILON)
    return centred * factor, factor


def turned(spectrum):
    return jnp.stack([-spectrum[1], spectrum[0]])


def run_layer(stream, rows_all, keep, norm, early, late, hat, skip, tables, count, beside_rows, beside_product):
    gain, bias = norm
    waves, waves_back = tables
    length = waves.shape[1]
    xhat, factor = normalize(stream)
    if rows_all is None:
        own, wait = beside_rows((xhat * gain + bias).astype(BF))
        normed, wait = seq_rows(own, count, wait)
    else:
        normed, wait = (normalize(rows_all.astype(F32))[0] * gain + bias).astype(BF), ()
    w_value = early(wait)
    value_act, value_slope = gelu_parts(dot(normed, w_value, 1, 0))
    values = (value_act * keep).astype(BF)
    value_slope = (value_slope * keep).astype(BF)
    values, value_slope = together(values, value_slope)
    x_hat = dot(waves, values, 1, 0).astype(BF)
    k_cos, k_sin = hat()
    x_cos, x_sin = x_hat[:length].astype(F32), x_hat[length:].astype(F32)
    y_hat = jnp.concatenate([k_cos * x_cos - k_sin * x_sin, k_cos * x_sin + k_sin * x_cos], 0).astype(BF)
    mixes = dot(waves_back, y_hat, 1, 0) * (1.0 / length) + skip * values.astype(F32)
    width = mixes.shape[1] // 2
    product = (mixes[:, :width] * mixes[:, width:]).astype(BF)
    product, mixes = together(product, mixes.astype(BF))
    product, wait = beside_product(product)
    products, wait = seq_gather(product, count, wait)
    w_gate, w_mix, w_out = late(wait)
    gate_act, gate_slope = gelu_parts(dot(normed, w_gate, 1, 0))
    update = dot(products[0], w_mix[0], 1, 0)
    for member in range(1, count):
        update = update + dot(products[member], w_mix[member], 1, 0)
    mixed = (update * gate_act).astype(BF)
    gate_back = (update * gate_slope).astype(BF)
    mixed, gate_act, gate_back = together(mixed, gate_act.astype(BF), gate_back)
    result = stream + seq_reduce_rows(dot(mixed, w_out, 1, 0), count)
    saved = (
        xhat,
        factor,
        normed,
        gate_act,
        gate_back,
        value_slope,
        together(values)[0],
        x_hat,
        mixes,
        products,
        mixed,
    )
    return result, saved


def back_gate(grad_stream, saved, late, count, wait):
    w_gate, w_mix, w_out = late
    xhat, factor, normed, gate_act, gate_back, value_slope, values, x_hat, mixes, products, mixed = saved
    out_low, wait = seq_rows(grad_stream, count, wait)
    grad_mixed = dot(out_low, w_out, 1, 1)
    update_low = (grad_mixed * gate_act.astype(F32)).astype(BF)
    gate_grad = (grad_mixed * gate_back.astype(F32)).astype(BF)
    update_low, gate_grad = together(update_low, gate_grad)
    width = products[0].shape[1]
    model = out_low.shape[1]
    blocks = dict(enumerate(dot(update_low, w_mix[m], 1, 1) for m in range(count)))
    for bit in bits_of(count):
        for member in sorted(blocks, reverse=True):
            if member & bit:
                sent = blocks.pop(member).astype(BF)
                if member == count // 2:
                    sent, update_low, gate_grad, out_low = together(sent, update_low, gate_grad, out_low)
                blocks[member ^ bit] = add_half(blocks[member ^ bit], swap(sent, "seq", count, bit), F32)
    product_low = blocks[0]
    grad_out = [
        dot(mixed, out_low[:, j * width : (j + 1) * width], 0, 0).astype(BF) for j in range(model // width)
    ]
    grad_mix = [dot(products[m], update_low, 0, 0).astype(BF) for m in range(count)]
    grad_gate = dot(normed, gate_grad, 0, 0).astype(BF)
    gate_part = dot(gate_grad, w_gate, 1, 1)
    return product_low.astype(BF), gate_part, (grad_gate, grad_mix, grad_out), wait


def back_convolution(product_low, saved, hat, skip, tables):
    xhat, factor, normed, gate_act, gate_back, value_slope, values, x_hat, mixes, products, mixed = saved
    waves, waves_back = tables
    length = waves.shape[1]
    width = product_low.shape[1]
    back = jnp.concatenate([product_low * mixes[:, width:], product_low * mixes[:, :width]], 1)
    g_hat = dot(waves, back, 1, 0).astype(BF)
    k_cos, k_sin = hat
    g_cos, g_sin = g_hat[:length].astype(F32), g_hat[length:].astype(F32)
    y_hat = jnp.concatenate([k_cos * g_cos + k_sin * g_sin, k_cos * g_sin - k_sin * g_cos], 0).astype(BF)
    grad_values = dot(waves_back, y_hat, 1, 0) * (1.0 / length) + skip * back.astype(F32)
    x_cos, x_sin = x_hat[:length].astype(F32), x_hat[length:].astype(F32)
    sign = jnp.concatenate([jnp.ones((width,), F32), -jnp.ones((width,), F32)])
    kern_hat = (
        (g_cos * x_cos + g_sin * x_sin).astype(BF),
        ((g_sin * x_cos - g_cos * x_sin) * sign).astype(BF),
    )
    grad_skip = jnp.sum(back.astype(F32) * values.astype(F32), axis=0)
    value_grad = (grad_values.astype(BF).astype(F32) * value_slope.astype(F32)).astype(BF)
    return value_grad, kern_hat, grad_skip


def back_norm(grad_stream, grad_normed, saved, gain):
    xhat, factor = saved[:2]
    norm_terms = jnp.stack([jnp.sum(grad_normed * xhat, 0), jnp.sum(grad_normed, 0)])
    inner = grad_normed * gain
    slope = jnp.mean(inner, axis=-1, keepdims=True)
    tilt = jnp.mean(inner * xhat, axis=-1, keepdims=True)
    return grad_stream + (inner - slope - xhat * tilt) * factor, norm_terms


def shards(tokens, lengths, cotangent, w_gate, w_value, w_mix, w_out, ln_gain, ln_bias, ssm_coef, ssm_rate, ssm_skip):
    dp = lax.axis_size("dp")
    count = lax.axis_size("seq")
    rows, model = tokens.shape
    length = rows * count
    depth, in_rows, gate_width = w_gate.shape
    mix_rows = w_mix.shape[1]
    width = ssm_coef.shape[2]
    states = ssm_coef.shape[3]
    share = gate_width // (dp * count)
    out_parts = model // width
    order = [lax.axis_index("seq") ^ m for m in range(count)]
    keep = (jnp.arange(length, dtype=jnp.int32) < lengths[0]).astype(F32)[:, None]
    table = wave_table(length)
    waves = jnp.asarray(table)
    tables = (waves, jnp.asarray(np.ascontiguousarray(table.T)))

    def by_column(weight):
        cut = weight.reshape(weight.shape[0], dp, count, share)
        return cut.transpose(2, 0, 1, 3).reshape(count, weight.shape[0], width)

    def value_columns(layer):
        cut = w_value[layer].reshape(in_rows, 2, count, width).transpose(2, 1, 0, 3)
        return cut.reshape(count, 2 * in_rows, width)

    norm_rows = jnp.stack([ln_gain, ln_bias], 1).reshape(2 * depth, in_rows)
    norm_rows = jnp.pad(norm_rows, ((0, 16 - 2 * depth), (0, width - in_rows)))
    first = jnp.concatenate([value_columns(0), jnp.broadcast_to(norm_rows, (count,) + norm_rows.shape)], 1)
    first, tokens = together(first, tokens)
    first = lax.all_to_all(first, "seq", 0, 0, tiled=True)
    rows_all, first = seq_rows(tokens, count, first)
    pieces = [by_column(w_gate[0]), by_column(w_mix[0])]
    for layer in range(1, depth):
        pieces += [value_columns(layer), by_column(w_gate[layer]), by_column(w_mix[layer])]
    sizes = [piece.shape[1] for piece in pieces]
    first, rest = together(first, jnp.concatenate(pieces, 1))

    coefs = ssm_coef.reshape(depth, width, 2 * states)
    rates = ssm_rate.reshape(depth, width, 2 * states)
    skips = ssm_skip.reshape(depth, 2 * width)
    sign = jnp.concatenate([jnp.ones((1, width), F32), -jnp.ones((1, width), F32)], 1)
    table_parts = 2 * width // channel_block(2 * width)

    def make_tables(layer, parts_made, hat, tie):
        rate, tie = together(rates, tie)
        for part in parts_made:
            hat = spectra(coefs, rate, sign, waves, layer, part, hat)
        return hat, tie

    def flat(piece):
        return piece.reshape(-1, width)

    def value_sides(piece):
        return [flat(piece[:, side * in_rows : (side + 1) * in_rows]) for side in range(2)]

    def out_sides(layer):
        return [w_out[layer][:, j * width : (j + 1) * width] for j in range(out_parts)]

    norm_piece = first[:, 2 * in_rows :, :in_rows].transpose(1, 0, 2).reshape(16, count * in_rows)
    norm_piece = jnp.pad(norm_piece, ((0, 0), (0, -(count * in_rows) % width)))
    sides = value_sides(first)
    n_in = count * in_rows
    pair = [jnp.concatenate([sides[0], flat(norm_piece)], 0), sides[1]]
    paths = [far_first(dp), y_first(dp)[:1] + far_first(dp)[:-1]]
    pair, rest = together(pair, rest)
    rest = lax.all_to_all(rest, "seq", 0, 0, tiled=True)
    rest = jnp.split(rest, np.cumsum(sizes)[:-1].tolist(), axis=1)
    late_block = jnp.concatenate([flat(rest[0]), flat(rest[1])] + out_sides(0), 0)
    done = [[], []]
    hat = ()
    for step in range(len(bits_of(dp))):
        others = [swap(block, "dp", dp, path[step]) for block, path in zip(pair, paths)]
        if step < table_parts:
            hat, pair = make_tables(0, [step], hat, pair)
            others, hat = together(others, hat)
        if step == 1:
            others, late_block = together(others, late_block)
        for j in range(2):
            done[j] = sorted(done[j] + [paths[j][step]], reverse=True)
            pair[j] = join(pair[j], others[j], "dp", paths[j][step], done[j])
    hat, pair = make_tables(0, range(len(bits_of(dp)), table_parts), hat, pair)
    hats = [hat]
    pair, rows_all = together(pair, rows_all)
    side_a, side_b = [block.reshape((dp,) + block.shape[-2:]) for block in pair]
    norms = side_a[:, n_in:].reshape(dp, 16, -1)[:, : 2 * depth, :n_in]
    norms = norms.transpose(1, 0, 2).reshape(depth, 2, model).astype(F32)

    def value_weight(side_a, side_b):
        return jnp.concatenate([side_a.reshape(model, width), side_b.reshape(model, width)], 1)

    def mix_weight(block):
        block = block.reshape(count, width, width)
        return [lax.dynamic_index_in_dim(block, order[m], 0, keepdims=False) for m in range(count)]

    def out_weight(block):
        cut = block.reshape(dp, out_parts, mix_rows, width).transpose(0, 2, 1, 3)
        return cut.reshape(dp * mix_rows, model)

    early = [(value_weight(side_a[:, :n_in], side_b), norms[0, 0], norms[0, 1])]
    got_late = lax.all_gather(late_block, "dp", axis=0)

    def late_weights(got):
        gate, mix, out = jnp.split(got, [n_in, n_in + count * mix_rows], axis=1)
        return gate.reshape(model, width), mix_weight(mix), out_weight(out)

    def layer_block(layer):
        value, gate, mix = rest[3 * layer - 1 : 3 * layer + 2]
        return jnp.concatenate(value_sides(value) + [flat(gate), flat(mix)] + out_sides(layer), 0)

    got_layers = [None] + [lax.all_gather(layer_block(layer), "dp", axis=0) for layer in range(1, depth)]

    late = []
    stream = tokens.astype(F32)
    kept = []
    for layer in range(depth):

        def beside_rows(own):
            return own, got_layers[layer]

        def early_weights(got):
            if layer:
                side_a, side_b, got = jnp.split(got, [n_in, 2 * n_in], axis=1)
                early.append((value_weight(side_a, side_b), norms[layer, 0], norms[layer, 1]))
                late.append(late_weights(got))
            return early[layer][0]

        def beside_product(product):
            hat = ()
            if layer + 1 < depth:
                hat, product = make_tables(layer + 1, range(table_parts), (), product)
            return product, (() if layer else got_late, hat)

        def later_weights(wait):
            if not layer:
                late.append(late_weights(wait[0]))
            hats.append(wait[1])
            return late[layer]

        stream, saved = run_layer(
            stream, None if layer else rows_all, keep, norms[layer], early_weights, later_weights,
            lambda: hats[layer], skips[layer], tables, count, beside_rows, beside_product,
        )
        kept.append(saved)

    def owner_pieces(rows_list):
        pieces = [piece.reshape(count, -1, width) for piece in rows_list]
        return jnp.concatenate(pieces, 1), np.cumsum([piece.shape[1] for piece in pieces])[:-1].tolist()

    def natural(blocks):
        whole = jnp.zeros((count,) + blocks[0].shape, blocks[0].dtype)
        for member, block in enumerate(blocks):
            whole = lax.dynamic_update_index_in_dim(whole, block, order[member], 0)
        return whole

    grad_stream = cotangent.astype(F32)
    norm_grads = [None] * depth
    ssm_grads = [None] * depth
    held = [None] * depth
    kern_hat = None
    turn = lax.axis_index("seq") * (dp // count)
    paths = [y_first(dp), z_first(dp), y_first(dp)]
    turns = [turn, 0, 0]

    def sent_dp(pairs, at):
        return [
            (pair[0], swap(pair[1], "dp", dp, path[step])) for pair, path, step in zip(pairs, paths, at)
        ]

    def next_dp(pairs, at):
        return [
            cut_half(add_half(*pair, BF), "dp", dp, path[step], side)
            for pair, path, side, step in zip(pairs, paths, turns, at)
        ]

    for layer in reversed(range(depth)):
        low = grad_stream.astype(BF)
        wait = ()
        if kern_hat is not None:
            low, kern_hat = together(low, kern_hat)
            wait = state_grads(coefs, rates, *kern_hat, waves, layer + 1)
        product_low, gate_part, terms, wait = back_gate(low, kept[layer], late[layer], count, wait)
        if kern_hat is not None:
            ssm_grads[layer + 1] += wait
        grad_gate, grad_mix, grad_out = terms
        others = [grad_gate.reshape(dp, n_in, width)] + [g.reshape(dp, mix_rows, width) for g in grad_out]
        if not layer:
            blocks = [jnp.stack(grad_mix).reshape(dp, count * mix_rows, width), jnp.concatenate(others, 1)]
            moving = [
                cut_half(bit_blocks(block, dp), "dp", dp, path[0], side)
                for block, path, side in zip(blocks, paths, turns)
            ]
            product_low, moving = together(product_low, moving)
            moving = sent_dp(moving, (0, 0))
        value_grad, kern_hat, grad_skip = back_convolution(product_low, kept[layer], hats[layer], skips[layer], tables)
        ssm_grads[layer] = (grad_skip,)
        if not layer:
            value_grad, moving = together(value_grad, moving)
            moving = next_dp(moving, (1, 1))
        normed = kept[layer][2]
        values = dot(normed, value_grad, 0, 0).astype(BF).reshape(dp, n_in, 2 * width)
        parts = dot(value_grad, early[layer][0], 1, 1) + gate_part
        sums = bit_blocks(parts.reshape(count, rows, model), count)
        if layer:
            block = [natural(grad_mix).reshape(dp, count * mix_rows, width)] + others
            block = jnp.concatenate(block + [values[:, :, :width], values[:, :, width:]], 1)
            held[layer] = lax.psum_scatter(block, "dp", scatter_dimension=0, tiled=False)
        else:
            moving.append(cut_half(bit_blocks(values, dp), "dp", dp, paths[2][0]))
        for step, bit in enumerate(bits_of(count)):
            held_rows, sent = cut_half(sums, "seq", count, bit)
            if step == 1 and not layer:
                sent, moving, kern_hat = together(sent, moving, kern_hat)
                came = swap(sent, "seq", count, bit)
                moving = sent_dp(moving, (1, 1, 0))
                last = state_grads(coefs, rates, *kern_hat, waves, 0)
                came, moving, last = together(came, moving, last)
                ssm_grads[0] += last
            else:
                came = swap(sent, "seq", count, bit)
            sums = add_half(held_rows, came, F32)
        grad_normed = sums.reshape(rows, model)
        grad_stream, norm_grads[layer] = back_norm(grad_stream, grad_normed, kept[layer], early[layer][1])

    own = width // dp
    both = 2 * states
    norm_all = jnp.stack(norm_grads).reshape(2 * depth, dp, n_in).transpose(1, 0, 2)
    lanes = -(-max(2 * own, n_in) // both) * both
    skip_rows = jnp.stack([g[0].reshape(dp, 2 * own) for g in ssm_grads], 1)
    skip_rows = jnp.concatenate(
        [
            jnp.pad(skip_rows, ((0, 0), (0, 0), (0, lanes - 2 * own))),
            jnp.pad(norm_all, ((0, 0), (0, 16 - 3 * depth), (0, lanes - n_in))),
        ],
        1,
    ).reshape(dp, -1, both)
    states_all = jnp.stack([g[j].reshape(dp, own, both) for g in ssm_grads for j in (1, 2)], 1).astype(BF)
    ssm_rows = jnp.concatenate([states_all.reshape(dp, 2 * depth * own, both), skip_rows.astype(BF)], 1)

    sums = [add_half(*pair, BF) for pair in moving] + [bit_blocks(ssm_rows, dp)]
    paths = [paths[0][2:], paths[1][2:], paths[2][1:], y_first(dp)]
    turns = turns + [0]

    def flat_sum(j):
        return sums[j].reshape(sums[j].shape[-2:])

    first_round = True
    while any(paths):
        active = [j for j, path in enumerate(paths) if path]
        pairs = [cut_half(sums[j], "dp", dp, paths[j][0], turns[j]) for j in active]
        pairs = lax.optimization_barrier(pairs)
        pairs = [(pair[0], swap(pair[1], "dp", dp, paths[j][0])) for j, pair in zip(active, pairs)]
        if first_round:
            pairs, held = together(pairs, held)
            first_round = False
        else:
            pairs = lax.optimization_barrier(pairs)
        for j, pair in zip(active, pairs):
            sums[j] = add_half(*pair, BF)
            paths[j] = paths[j][1:]
    own_sum = flat_sum(3)
    norm_own = own_sum[2 * depth * own :].reshape(16, lanes)[depth : 3 * depth, :n_in]
    norm_own = norm_own.reshape(2 * depth, count, in_rows).transpose(1, 0, 2)
    norm_own = jnp.pad(norm_own, ((0, 0), (0, 16 - 2 * depth), (0, width - in_rows)))
    cuts = np.cumsum([count * mix_rows, n_in, out_parts * mix_rows, n_in]).tolist()
    value_sums = flat_sum(2)
    rows_list = [flat_sum(1)[:n_in], flat_sum(0), value_sums[:, :width], value_sums[:, width:]]
    outs = [flat_sum(1)[n_in:]]
    for layer in range(1, depth):
        mix, gate, out, side_a, side_b = jnp.split(held[layer], cuts, axis=0)
        outs.append(out)
        rows_list += [gate, mix, side_a, side_b]
    last, last_cuts = owner_pieces(rows_list + [norm_own.reshape(count * 16, width)])
    own_sum, last = together(own_sum, last)
    last = lax.all_to_all(last, "seq", 0, 0, tiled=True)
    ssm_sum, last = gather_bits(own_sum, "dp", dp, far_first(dp), last)
    ssm_sum = ssm_sum.astype(F32)
    back_parts = jnp.split(last, last_cuts, axis=1)
    norm_came = back_parts.pop()
    back = back_parts
    norm_sum = jnp.sum(norm_came[:, : 2 * depth, :in_rows].astype(F32), 0).reshape(depth, 2, in_rows)

    def columns(block):
        cut = block.reshape(count, -1, dp, share).transpose(1, 2, 0, 3)
        return cut.reshape(-1, gate_width).astype(F32)

    def value_share(sides):
        sides = jnp.stack(sides, 0)
        return sides.transpose(2, 0, 1, 3).reshape(in_rows, 2 * count * width).astype(F32)

    def out_share(block):
        return block.reshape(out_parts, mix_rows, width).transpose(1, 0, 2).reshape(mix_rows, model).astype(F32)

    gates, mixes, values = [], [], []
    for layer in range(depth):
        gate, mix, side_a, side_b = back[4 * layer : 4 * layer + 4]
        gates.append(columns(gate))
        mixes.append(columns(mix))
        values.append(value_share([side_a, side_b]))
    outs = [out_share(out) for out in outs]

    state_sum = ssm_sum[:, : 2 * depth * own].reshape(dp, depth, 2, own, both).transpose(1, 2, 0, 3, 4)
    coef_sum, rate_sum = state_sum[:, 0], state_sum[:, 1]
    skip_sum = ssm_sum[:, 2 * depth * own :].reshape(dp, 16, lanes)[:, :depth, : 2 * own].transpose(1, 0, 2)
    return (
        stream,
        grad_stream,
        jnp.stack(gates),
        jnp.stack(values),
        jnp.stack(mixes),
        jnp.stack(outs),
        norm_sum[:, 0],
        norm_sum[:, 1],
        coef_sum.reshape(ssm_coef.shape),
        rate_sum.reshape(ssm_rate.shape),
        skip_sum.reshape(ssm_skip.shape),
    )


def solution(mesh):
    in_specs = (
        P(("dp", "seq"), None),
        P("dp"),
        P(("dp", "seq"), None),
        P(None, ("dp", "seq"), None),
        P(None, ("dp", "seq"), None),
        P(None, ("dp", "seq"), None),
        P(None, ("dp", "seq"), None),
        P(None, ("dp", "seq")),
        P(None, ("dp", "seq")),
        P(None, None, "seq", None),
        P(None, None, "seq", None),
        P(None, None, "seq"),
    )
    out_specs = (
        P(("dp", "seq"), None),
        P(("dp", "seq"), None),
        P(None, ("dp", "seq"), None),
        P(None, ("dp", "seq"), None),
        P(None, ("dp", "seq"), None),
        P(None, ("dp", "seq"), None),
        P(None, ("dp", "seq")),
        P(None, ("dp", "seq")),
        P(None, None, "seq", None),
        P(None, None, "seq", None),
        P(None, None, "seq"),
    )
    return jax.shard_map(shards, mesh=mesh, in_specs=in_specs, out_specs=out_specs, check_vma=False)
```

```python
from functools import partial

import numpy as np

import jax
import jax.numpy as jnp
from jax import lax
from jax.experimental import pallas as pl
from jax.experimental.layout import Layout, with_layout_constraint
from jax.experimental.pallas import tpu as pltpu
from jax.sharding import PartitionSpec as P

EPSILON = 1e-05
BF = jnp.bfloat16
F32 = jnp.float32
LANES = 128


def dot(left, right, left_dim, right_dim):
    return lax.dot_general(
        left, right, (((left_dim,), (right_dim,)), ((), ())), preferred_element_type=F32
    )


def wave_table(length):
    step = np.arange(length, dtype=np.int64)
    phase = ((2 * step[:, None] + 1) * step[None, :]) % (4 * length)
    angle = phase * (np.pi / (2 * length))
    return np.concatenate([np.cos(angle), np.sin(angle)], 0).astype(jnp.bfloat16)


def decay_tiles(rate):
    rows = lax.broadcasted_iota(jnp.int32, (8, LANES), 0).astype(F32)
    tiles = [jnp.exp(-rate * rows)]
    step = jnp.exp(-8.0 * jnp.broadcast_to(rate, (8, LANES)))
    while len(tiles) < LANES // 8:
        tiles = tiles + [tile * step for tile in tiles]
        step = step * step
    return tiles


def block_decays(rate, count):
    starts = lax.broadcasted_iota(jnp.int32, (count, LANES), 0).astype(F32) * float(LANES)
    return starts, jnp.exp(-rate * starts)


def spectra_kernel(unroll, rate_ref, coef_ref, sign_ref, wave_home, *refs):
    cos_ref, sin_ref, kern_ref, flat_ref, wave_ref, sem = refs[-6:]
    pairs = rate_ref.shape[0]
    length = wave_ref.shape[1]
    load = pltpu.make_async_copy(wave_home, wave_ref, sem)
    load.start()
    count = length // LANES
    lower = lax.broadcasted_iota(jnp.int32, (count, LANES), 1) < LANES // 2

    def pair(step, carry):
        for offset in range(unroll):
            index = step * unroll + offset
            rate = rate_ref[pl.ds(index, 1), :]
            near = jnp.concatenate(decay_tiles(rate), 0).astype(BF)
            far = block_decays(rate, count)[1] * (coef_ref[pl.ds(index, 1), :] * rate)
            left = jnp.concatenate([jnp.where(lower, far, 0.0), jnp.where(lower, 0.0, far)], 0)
            place = pl.ds(pl.multiple_of(index * 2 * count, 2 * count), 2 * count)
            kern_ref[place, :] = dot(left.astype(BF), near, 1, 1)
        return carry

    lax.fori_loop(0, pairs // unroll, pair, 0)
    for part in range(count):
        flat_ref[:, part * LANES : (part + 1) * LANES] = kern_ref[
            pl.ds(part, 2 * pairs, stride=count), :
        ].astype(BF)
    load.wait()
    chunk = 256
    for part in range(length // chunk):
        rows = slice(part * chunk, (part + 1) * chunk)
        cos_ref[rows, :] = dot(wave_ref[rows, :], flat_ref[...], 1, 1).astype(BF)
        sines = dot(wave_ref[length + part * chunk : length + (part + 1) * chunk, :], flat_ref[...], 1, 1)
        sin_ref[rows, :] = (sines * sign_ref[...]).astype(BF)


def channel_block(channels):
    return 256 if channels % 256 == 0 else channels


def unroll_of(pairs):
    return 16 if pairs % 16 == 0 else 8


def table_bytes(wave):
    return 2 * wave.shape[0] * wave.shape[1] + 12 * 2**20


def whole_table(wave):
    return pl.BlockSpec(wave.shape, lambda j: (0, 0), pipeline_mode=pl.Buffered(1))


def spectra(coef, rate, sign, wave, layer, part, earlier):
    channels = 2 * coef.shape[1]
    length = wave.shape[1]
    block = channel_block(channels)
    rows = pl.BlockSpec((None, block // 2, LANES), lambda j: (layer, part, 0))
    lanes = pl.BlockSpec((length, block), lambda j: (0, part))
    shape = jax.ShapeDtypeStruct((length, channels), BF)
    return pl.pallas_call(
        partial(spectra_kernel, unroll_of(block // 2)),
        out_shape=(shape, shape),
        grid=(1,),
        in_specs=[
            rows,
            rows,
            pl.BlockSpec((1, block), lambda j: (0, part)),
            pl.BlockSpec(memory_space=pltpu.HBM),
        ]
        + [pl.BlockSpec(memory_space=pl.ANY)] * len(earlier),
        out_specs=(lanes, lanes),
        scratch_shapes=[
            pltpu.VMEM((block * length // LANES, LANES), F32),
            pltpu.VMEM((block, length), BF),
            pltpu.VMEM(wave.shape, BF),
            pltpu.SemaphoreType.DMA,
        ],
        input_output_aliases={4 + j: j for j in range(len(earlier))},
        compiler_params=pltpu.CompilerParams(vmem_limit_bytes=table_bytes(wave)),
        cost_estimate=pl.CostEstimate(
            flops=12 * length * length * block,
            bytes_accessed=4 * length * length + 4 * length * block,
            transcendentals=0,
        ),
        name="spectra",
    )(rate, coef, sign, wave, *earlier)


def state_grads_kernel(
    unroll, rate_ref, coef_ref, cos_ref, sin_ref, wave_ref, coef_out, rate_out, turned_ref, kern_ref
):
    pairs = rate_ref.shape[0]
    length = wave_ref.shape[1]
    count = length // LANES
    lower = lax.broadcasted_iota(jnp.int32, (count, LANES), 1) < LANES // 2
    row = lax.broadcasted_iota(jnp.int32, (8, LANES), 0).astype(F32)
    turned_ref[:, :length] = cos_ref[...].T
    turned_ref[:, length:] = sin_ref[...].T
    chunk = 256
    for part in range(length // chunk):
        got = dot(turned_ref[...], wave_ref[:, part * chunk : (part + 1) * chunk], 1, 0)
        for side in range(chunk // LANES):
            place = pl.ds(part * (chunk // LANES) + side, 2 * pairs, stride=count)
            kern_ref[place, :] = got[:, side * LANES : (side + 1) * LANES]

    def pair(step, carry):
        for offset in range(unroll):
            index = step * unroll + offset
            rate = rate_ref[pl.ds(index, 1), :]
            coef = coef_ref[pl.ds(index, 1), :]
            tiles = decay_tiles(rate)
            near = jnp.concatenate(tiles, 0).astype(BF)
            lagged = jnp.concatenate([tile * (row + 8.0 * j) for j, tile in enumerate(tiles)], 0)
            place = pl.ds(pl.multiple_of(index * 2 * count, 2 * count), 2 * count)
            both = jnp.concatenate([near, lagged.astype(BF)], 1)
            got = dot(kern_ref[place, :].astype(BF), both, 1, 0)
            plain = jnp.where(lower, got[:count, :LANES], got[count:, :LANES])
            first = jnp.where(lower, got[:count, LANES:], got[count:, LANES:])
            starts, far = block_decays(rate, count)
            total = jnp.sum(far * plain, axis=0, keepdims=True)
            moment = jnp.sum(far * (starts * plain + first), axis=0, keepdims=True)
            coef_out[pl.ds(index, 1), :] = rate * total * (1.0 / length)
            rate_out[pl.ds(index, 1), :] = coef * (total - rate * moment) * (1.0 / length)
        return carry

    lax.fori_loop(0, pairs // unroll, pair, 0)


def state_grads(coef, rate, cosines, sines, wave, layer):
    channels = 2 * coef.shape[1]
    length = wave.shape[1]
    block = channel_block(channels)
    rows = pl.BlockSpec((None, block // 2, LANES), lambda j: (layer, j, 0))
    made = pl.BlockSpec((block // 2, LANES), lambda j: (j, 0))
    lanes = pl.BlockSpec((length, block), lambda j: (0, j))
    shape = jax.ShapeDtypeStruct(coef.shape[1:], F32)
    return pl.pallas_call(
        partial(state_grads_kernel, unroll_of(block // 2)),
        out_shape=(shape, shape),
        grid=(channels // block,),
        in_specs=[rows, rows, lanes, lanes, whole_table(wave)],
        out_specs=(made, made),
        scratch_shapes=[
            pltpu.VMEM((block, 2 * length), BF),
            pltpu.VMEM((block * length // LANES, LANES), F32),
        ],
        compiler_params=pltpu.CompilerParams(vmem_limit_bytes=table_bytes(wave)),
        cost_estimate=pl.CostEstimate(
            flops=12 * length * length * channels,
            bytes_accessed=4 * length * length + 4 * length * channels,
            transcendentals=0,
        ),
        name="state_grads",
    )(rate, coef, cosines, sines, wave)


def pairs_of(count, bit):
    return [(i, i ^ bit) for i in range(count)]


def seq_gather(block, count, wait):
    blocks = {0: block}
    bit = count // 2
    while bit:
        for member in list(blocks):
            blocks[member ^ bit] = lax.ppermute(blocks[member], "seq", pairs_of(count, bit))
        if bit == count // 2:
            blocks[bit], wait = together(blocks[bit], wait)
        bit //= 2
    return [blocks[m] for m in range(count)], wait


def seq_rows(block, count, wait):
    whole, wait = gather_bits(block, "seq", count, far_first(count), wait)
    return row_major(whole.reshape(count * block.shape[0], block.shape[1])), wait


def seq_reduce_rows(whole, count):
    blocks = whole.reshape(count, -1, whole.shape[1])
    return reduce_bits(blocks, "seq", count, bits_of(count), F32)


def row_major(array):
    return with_layout_constraint(array, Layout(tuple(range(array.ndim))))


def bits_of(count):
    return [1 << j for j in range(count.bit_length() - 1)]


def far_first(count):
    return bits_of(count)[::-1]


def y_first(count):
    return bits_of(count)


def z_first(count):
    return bits_of(count)[1:] + bits_of(count)[:1]


def swap(block, axis, count, bit):
    return lax.ppermute(block, axis, pairs_of(count, bit))


def join(block, other, axis, bit, done):
    upper = (lax.axis_index(axis) & bit) != 0
    pair = [jnp.where(upper, other, block), jnp.where(upper, block, other)]
    return jnp.stack(pair, done.index(bit))


def gather_bits(block, axis, count, sequence, wait=()):
    done = []
    for bit in sequence:
        other = swap(block, axis, count, bit)
        if not done:
            other, wait = together(other, wait)
        done = sorted(done + [bit], reverse=True)
        block = join(block, other, axis, bit, done)
    return block.reshape((count,) + block.shape[len(done) :]), wait


def cut_half(blocks, axis, count, bit, turn=0):
    level = far_first(count).index(bit)
    side = ((lax.axis_index(axis) ^ turn) // bit) % 2
    sent = lax.dynamic_slice_in_dim(blocks, 1 - side, 1, level).astype(BF)
    return lax.dynamic_slice_in_dim(blocks, side, 1, level), sent


def add_half(held, came, kind):
    return (held.astype(F32) + came.astype(F32)).astype(kind)


def bit_blocks(blocks, count):
    return blocks.reshape((2,) * len(bits_of(count)) + blocks.shape[1:])


def reduce_bits(blocks, axis, count, sequence, kind):
    blocks = bit_blocks(blocks, count)
    for bit in sequence:
        held, sent = cut_half(blocks, axis, count, bit)
        blocks = add_half(held, swap(sent, axis, count, bit), kind)
    return blocks.reshape(blocks.shape[len(bits_of(count)) :])


def together(*arrays):
    return lax.optimization_barrier(arrays)


def gelu_parts(pre):
    share = 0.5 * (1.0 + lax.erf(pre * np.float32(np.sqrt(0.5))))
    slope = share + pre * (jnp.exp(-0.5 * pre * pre) * np.float32(1.0 / np.sqrt(2.0 * np.pi)))
    return pre * share, slope


def normalize(stream):
    centre = jnp.mean(stream, axis=-1, keepdims=True)
    centred = stream - centre
    spread = jnp.mean(centred * centred, axis=-1, keepdims=True)
    factor = lax.rsqrt(spread + EPSILON)
    return centred * factor, factor


def turned(spectrum):
    return jnp.stack([-spectrum[1], spectrum[0]])


def run_layer(stream, rows_all, keep, norm, early, late, hat, skip, tables, count, beside_rows, beside_product):
    gain, bias = norm
    waves, waves_back = tables
    length = waves.shape[1]
    xhat, factor = normalize(stream)
    if rows_all is None:
        own, wait = beside_rows((xhat * gain + bias).astype(BF))
        normed, wait = seq_rows(own, count, wait)
    else:
        normed, wait = (normalize(rows_all.astype(F32))[0] * gain + bias).astype(BF), ()
    w_value = early(wait)
    value_act, value_slope = gelu_parts(dot(normed, w_value, 1, 0))
    values = (value_act * keep).astype(BF)
    value_slope = (value_slope * keep).astype(BF)
    values, value_slope = together(values, value_slope)
    x_hat = dot(waves, values, 1, 0).astype(BF)
    k_cos, k_sin = hat()
    x_cos, x_sin = x_hat[:length].astype(F32), x_hat[length:].astype(F32)
    y_hat = jnp.concatenate([k_cos * x_cos - k_sin * x_sin, k_cos * x_sin + k_sin * x_cos], 0).astype(BF)
    mixes = dot(waves_back, y_hat, 1, 0) * (1.0 / length) + skip * values.astype(F32)
    width = mixes.shape[1] // 2
    product = (mixes[:, :width] * mixes[:, width:]).astype(BF)
    product, mixes = together(product, mixes.astype(BF))
    product, wait = beside_product(product)
    products, wait = seq_gather(product, count, wait)
    w_gate, w_mix, w_out = late(wait)
    gate_act, gate_slope = gelu_parts(dot(normed, w_gate, 1, 0))
    update = dot(products[0], w_mix[0], 1, 0)
    for member in range(1, count):
        update = update + dot(products[member], w_mix[member], 1, 0)
    mixed = (update * gate_act).astype(BF)
    gate_back = (update * gate_slope).astype(BF)
    mixed, gate_act, gate_back = together(mixed, gate_act.astype(BF), gate_back)
    result = stream + seq_reduce_rows(dot(mixed, w_out, 1, 0), count)
    saved = (
        xhat,
        factor,
        normed,
        gate_act,
        gate_back,
        value_slope,
        together(values)[0],
        x_hat,
        mixes,
        products,
        mixed,
    )
    return result, saved


def back_gate(grad_stream, saved, late, count, wait):
    w_gate, w_mix, w_out = late
    xhat, factor, normed, gate_act, gate_back, value_slope, values, x_hat, mixes, products, mixed = saved
    out_low, wait = seq_rows(grad_stream, count, wait)
    grad_mixed = dot(out_low, w_out, 1, 1)
    update_low = (grad_mixed * gate_act.astype(F32)).astype(BF)
    gate_grad = (grad_mixed * gate_back.astype(F32)).astype(BF)
    update_low, gate_grad = together(update_low, gate_grad)
    width = products[0].shape[1]
    model = out_low.shape[1]
    blocks = dict(enumerate(dot(update_low, w_mix[m], 1, 1) for m in range(count)))
    for bit in bits_of(count):
        for member in sorted(blocks, reverse=True):
            if member & bit:
                sent = blocks.pop(member).astype(BF)
                if member == count // 2:
                    sent, update_low, gate_grad, out_low = together(sent, update_low, gate_grad, out_low)
                blocks[member ^ bit] = add_half(blocks[member ^ bit], swap(sent, "seq", count, bit), F32)
    product_low = blocks[0]
    grad_out = [
        dot(mixed, out_low[:, j * width : (j + 1) * width], 0, 0).astype(BF) for j in range(model // width)
    ]
    grad_mix = [dot(products[m], update_low, 0, 0).astype(BF) for m in range(count)]
    grad_gate = dot(normed, gate_grad, 0, 0).astype(BF)
    gate_part = dot(gate_grad, w_gate, 1, 1)
    return product_low.astype(BF), gate_part, (grad_gate, grad_mix, grad_out), wait


def back_convolution(product_low, saved, hat, skip, tables):
    xhat, factor, normed, gate_act, gate_back, value_slope, values, x_hat, mixes, products, mixed = saved
    waves, waves_back = tables
    length = waves.shape[1]
    width = product_low.shape[1]
    back = jnp.concatenate([product_low * mixes[:, width:], product_low * mixes[:, :width]], 1)
    g_hat = dot(waves, back, 1, 0).astype(BF)
    k_cos, k_sin = hat
    g_cos, g_sin = g_hat[:length].astype(F32), g_hat[length:].astype(F32)
    y_hat = jnp.concatenate([k_cos * g_cos + k_sin * g_sin, k_cos * g_sin - k_sin * g_cos], 0).astype(BF)
    grad_values = dot(waves_back, y_hat, 1, 0) * (1.0 / length) + skip * back.astype(F32)
    x_cos, x_sin = x_hat[:length].astype(F32), x_hat[length:].astype(F32)
    sign = jnp.concatenate([jnp.ones((width,), F32), -jnp.ones((width,), F32)])
    kern_hat = (
        (g_cos * x_cos + g_sin * x_sin).astype(BF),
        ((g_sin * x_cos - g_cos * x_sin) * sign).astype(BF),
    )
    grad_skip = jnp.sum(back.astype(F32) * values.astype(F32), axis=0)
    value_grad = (grad_values.astype(BF).astype(F32) * value_slope.astype(F32)).astype(BF)
    return value_grad, kern_hat, grad_skip


def back_norm(grad_stream, grad_normed, saved, gain):
    xhat, factor = saved[:2]
    norm_terms = jnp.stack([jnp.sum(grad_normed * xhat, 0), jnp.sum(grad_normed, 0)])
    inner = grad_normed * gain
    slope = jnp.mean(inner, axis=-1, keepdims=True)
    tilt = jnp.mean(inner * xhat, axis=-1, keepdims=True)
    return grad_stream + (inner - slope - xhat * tilt) * factor, norm_terms


def shards(tokens, lengths, cotangent, w_gate, w_value, w_mix, w_out, ln_gain, ln_bias, ssm_coef, ssm_rate, ssm_skip):
    dp = lax.axis_size("dp")
    count = lax.axis_size("seq")
    rows, model = tokens.shape
    length = rows * count
    depth, in_rows, gate_width = w_gate.shape
    mix_rows = w_mix.shape[1]
    width = ssm_coef.shape[2]
    states = ssm_coef.shape[3]
    share = gate_width // (dp * count)
    out_parts = model // width
    order = [lax.axis_index("seq") ^ m for m in range(count)]
    keep = (jnp.arange(length, dtype=jnp.int32) < lengths[0]).astype(F32)[:, None]
    table = wave_table(length)
    waves = jnp.asarray(table)
    tables = (waves, jnp.asarray(np.ascontiguousarray(table.T)))

    def by_column(weight):
        cut = weight.reshape(weight.shape[0], dp, count, share)
        return cut.transpose(2, 0, 1, 3).reshape(count, weight.shape[0], width)

    def value_columns(layer):
        cut = w_value[layer].reshape(in_rows, 2, count, width).transpose(2, 1, 0, 3)
        return cut.reshape(count, 2 * in_rows, width)

    norm_rows = jnp.stack([ln_gain, ln_bias], 1).reshape(2 * depth, in_rows)
    norm_rows = jnp.pad(norm_rows, ((0, 16 - 2 * depth), (0, width - in_rows)))
    first = jnp.concatenate([value_columns(0), jnp.broadcast_to(norm_rows, (count,) + norm_rows.shape)], 1)
    first, tokens = together(first, tokens)
    first = lax.all_to_all(first, "seq", 0, 0, tiled=True)
    rows_all, first = seq_rows(tokens, count, first)
    pieces = [by_column(w_gate[0]), by_column(w_mix[0])]
    for layer in range(1, depth):
        pieces += [value_columns(layer), by_column(w_gate[layer]), by_column(w_mix[layer])]
    sizes = [piece.shape[1] for piece in pieces]
    first, rest = together(first, jnp.concatenate(pieces, 1))

    coefs = ssm_coef.reshape(depth, width, 2 * states)
    rates = ssm_rate.reshape(depth, width, 2 * states)
    skips = ssm_skip.reshape(depth, 2 * width)
    sign = jnp.concatenate([jnp.ones((1, width), F32), -jnp.ones((1, width), F32)], 1)
    table_parts = 2 * width // channel_block(2 * width)

    def make_tables(layer, parts_made, hat, tie):
        rate, tie = together(rates, tie)
        for part in parts_made:
            hat = spectra(coefs, rate, sign, waves, layer, part, hat)
        return hat, tie

    def flat(piece):
        return piece.reshape(-1, width)

    def value_sides(piece):
        return [flat(piece[:, side * in_rows : (side + 1) * in_rows]) for side in range(2)]

    def out_sides(layer):
        return [w_out[layer][:, j * width : (j + 1) * width] for j in range(out_parts)]

    norm_piece = first[:, 2 * in_rows :, :in_rows].transpose(1, 0, 2).reshape(16, count * in_rows)
    norm_piece = jnp.pad(norm_piece, ((0, 0), (0, -(count * in_rows) % width)))
    sides = value_sides(first)
    n_in = count * in_rows
    pair = [jnp.concatenate([sides[0], flat(norm_piece)], 0), sides[1]]
    paths = [far_first(dp), y_first(dp)[:1] + far_first(dp)[:-1]]
    pair, rest = together(pair, rest)
    rest = lax.all_to_all(rest, "seq", 0, 0, tiled=True)
    rest = jnp.split(rest, np.cumsum(sizes)[:-1].tolist(), axis=1)
    late_block = jnp.concatenate([flat(rest[0]), flat(rest[1])] + out_sides(0), 0)
    done = [[], []]
    hat = ()
    for step in range(len(bits_of(dp))):
        others = [swap(block, "dp", dp, path[step]) for block, path in zip(pair, paths)]
        if step < table_parts:
            hat, pair = make_tables(0, [step], hat, pair)
            others, hat = together(others, hat)
        if step == 1:
            others, late_block = together(others, late_block)
        for j in range(2):
            done[j] = sorted(done[j] + [paths[j][step]], reverse=True)
            pair[j] = join(pair[j], others[j], "dp", paths[j][step], done[j])
    hat, pair = make_tables(0, range(len(bits_of(dp)), table_parts), hat, pair)
    hats = [hat]
    pair, rows_all = together(pair, rows_all)
    side_a, side_b = [block.reshape((dp,) + block.shape[-2:]) for block in pair]
    norms = side_a[:, n_in:].reshape(dp, 16, -1)[:, : 2 * depth, :n_in]
    norms = norms.transpose(1, 0, 2).reshape(depth, 2, model).astype(F32)

    def value_weight(side_a, side_b):
        return jnp.concatenate([side_a.reshape(model, width), side_b.reshape(model, width)], 1)

    def mix_weight(block):
        block = block.reshape(count, width, width)
        return [lax.dynamic_index_in_dim(block, order[m], 0, keepdims=False) for m in range(count)]

    def out_weight(block):
        cut = block.reshape(dp, out_parts, mix_rows, width).transpose(0, 2, 1, 3)
        return cut.reshape(dp * mix_rows, model)

    early = [(value_weight(side_a[:, :n_in], side_b), norms[0, 0], norms[0, 1])]
    got_late = lax.all_gather(late_block, "dp", axis=0)

    def late_weights(got):
        gate, mix, out = jnp.split(got, [n_in, n_in + count * mix_rows], axis=1)
        return gate.reshape(model, width), mix_weight(mix), out_weight(out)

    def layer_block(layer):
        value, gate, mix = rest[3 * layer - 1 : 3 * layer + 2]
        return jnp.concatenate(value_sides(value) + [flat(gate), flat(mix)] + out_sides(layer), 0)

    got_layers = [None] + [lax.all_gather(layer_block(layer), "dp", axis=0) for layer in range(1, depth)]

    late = []
    stream = tokens.astype(F32)
    kept = []
    cut = min(2, table_parts)
    for layer in range(depth):

        def beside_rows(own):
            hat, own = make_tables(layer, range(cut, table_parts), hats[layer], own)
            return own, (got_layers[layer], hat)

        def early_weights(wait):
            if layer:
                got, hats[layer] = wait
                side_a, side_b, got = jnp.split(got, [n_in, 2 * n_in], axis=1)
                early.append((value_weight(side_a, side_b), norms[layer, 0], norms[layer, 1]))
                late.append(late_weights(got))
            return early[layer][0]

        def beside_product(product):
            hat = ()
            if layer + 1 < depth:
                hat, product = make_tables(layer + 1, range(cut), (), product)
            return product, (() if layer else late_weights(got_late), hat)

        def later_weights(wait):
            if not layer:
                late.append(wait[0])
            hats.append(wait[1])
            return late[layer]

        stream, saved = run_layer(
            stream, None if layer else rows_all, keep, norms[layer], early_weights, later_weights,
            lambda: hats[layer], skips[layer], tables, count, beside_rows, beside_product,
        )
        kept.append(saved)

    def owner_pieces(rows_list):
        pieces = [piece.reshape(count, -1, width) for piece in rows_list]
        return jnp.concatenate(pieces, 1), np.cumsum([piece.shape[1] for piece in pieces])[:-1].tolist()

    def natural(blocks):
        whole = jnp.zeros((count,) + blocks[0].shape, blocks[0].dtype)
        for member, block in enumerate(blocks):
            whole = lax.dynamic_update_index_in_dim(whole, block, order[member], 0)
        return whole

    grad_stream = cotangent.astype(F32)
    norm_grads = [None] * depth
    ssm_grads = [None] * depth
    held = [None] * depth
    kern_hat = None
    turn = lax.axis_index("seq") * (dp // count)
    paths = [y_first(dp), z_first(dp), y_first(dp)]
    turns = [turn, 0, 0]

    def sent_dp(pairs, at):
        return [
            (pair[0], swap(pair[1], "dp", dp, path[step])) for pair, path, step in zip(pairs, paths, at)
        ]

    def next_dp(pairs, at):
        return [
            cut_half(add_half(*pair, BF), "dp", dp, path[step], side)
            for pair, path, side, step in zip(pairs, paths, turns, at)
        ]

    for layer in reversed(range(depth)):
        low = grad_stream.astype(BF)
        wait = ()
        if kern_hat is not None:
            low, kern_hat = together(low, kern_hat)
            wait = state_grads(coefs, rates, *kern_hat, waves, layer + 1)
        product_low, gate_part, terms, wait = back_gate(low, kept[layer], late[layer], count, wait)
        if kern_hat is not None:
            ssm_grads[layer + 1] += wait
        grad_gate, grad_mix, grad_out = terms
        others = [grad_gate.reshape(dp, n_in, width)] + [g.reshape(dp, mix_rows, width) for g in grad_out]
        if not layer:
            blocks = [jnp.stack(grad_mix).reshape(dp, count * mix_rows, width), jnp.concatenate(others, 1)]
            moving = [
                cut_half(bit_blocks(block, dp), "dp", dp, path[0], side)
                for block, path, side in zip(blocks, paths, turns)
            ]
            product_low, moving = together(product_low, moving)
            moving = sent_dp(moving, (0, 0))
        value_grad, kern_hat, grad_skip = back_convolution(product_low, kept[layer], hats[layer], skips[layer], tables)
        ssm_grads[layer] = (grad_skip,)
        if not layer:
            moving = next_dp(moving, (1, 1))
        normed = kept[layer][2]
        values = dot(normed, value_grad, 0, 0).astype(BF).reshape(dp, n_in, 2 * width)
        parts = dot(value_grad, early[layer][0], 1, 1) + gate_part
        sums = bit_blocks(parts.reshape(count, rows, model), count)
        if layer:
            block = [natural(grad_mix).reshape(dp, count * mix_rows, width)] + others
            block = jnp.concatenate(block + [values[:, :, :width], values[:, :, width:]], 1)
            held[layer] = lax.psum_scatter(block, "dp", scatter_dimension=0, tiled=False)
        else:
            moving.append(cut_half(bit_blocks(values, dp), "dp", dp, paths[2][0]))
        for step, bit in enumerate(bits_of(count)):
            held_rows, sent = cut_half(sums, "seq", count, bit)
            if step == 1 and not layer:
                sent, moving, kern_hat = together(sent, moving, kern_hat)
                came = swap(sent, "seq", count, bit)
                moving = sent_dp(moving, (1, 1, 0))
                last = state_grads(coefs, rates, *kern_hat, waves, 0)
                came, moving, last = together(came, moving, last)
                ssm_grads[0] += last
            else:
                came = swap(sent, "seq", count, bit)
            sums = add_half(held_rows, came, F32)
        grad_normed = sums.reshape(rows, model)
        grad_stream, norm_grads[layer] = back_norm(grad_stream, grad_normed, kept[layer], early[layer][1])

    own = width // dp
    both = 2 * states
    norm_all = jnp.stack(norm_grads).reshape(2 * depth, dp, n_in).transpose(1, 0, 2)
    lanes = -(-max(2 * own, n_in) // both) * both
    skip_rows = jnp.stack([g[0].reshape(dp, 2 * own) for g in ssm_grads], 1)
    skip_rows = jnp.concatenate(
        [
            jnp.pad(skip_rows, ((0, 0), (0, 0), (0, lanes - 2 * own))),
            jnp.pad(norm_all, ((0, 0), (0, 16 - 3 * depth), (0, lanes - n_in))),
        ],
        1,
    ).reshape(dp, -1, both)
    states_all = jnp.stack([g[j].reshape(dp, own, both) for g in ssm_grads for j in (1, 2)], 1).astype(BF)
    ssm_rows = jnp.concatenate([states_all.reshape(dp, 2 * depth * own, both), skip_rows.astype(BF)], 1)

    sums = [add_half(*pair, BF) for pair in moving] + [bit_blocks(ssm_rows, dp)]
    paths = [paths[0][2:], paths[1][2:], paths[2][1:], y_first(dp)]
    turns = turns + [0]

    def flat_sum(j):
        return sums[j].reshape(sums[j].shape[-2:])

    first_round = True
    while any(paths):
        active = [j for j, path in enumerate(paths) if path]
        pairs = [cut_half(sums[j], "dp", dp, paths[j][0], turns[j]) for j in active]
        pairs = lax.optimization_barrier(pairs)
        pairs = [(pair[0], swap(pair[1], "dp", dp, paths[j][0])) for j, pair in zip(active, pairs)]
        if first_round:
            pairs, held = together(pairs, held)
            first_round = False
        else:
            pairs = lax.optimization_barrier(pairs)
        for j, pair in zip(active, pairs):
            sums[j] = add_half(*pair, BF)
            paths[j] = paths[j][1:]
    own_sum = flat_sum(3)
    norm_own = own_sum[2 * depth * own :].reshape(16, lanes)[depth : 3 * depth, :n_in]
    norm_own = norm_own.reshape(2 * depth, count, in_rows).transpose(1, 0, 2)
    norm_own = jnp.pad(norm_own, ((0, 0), (0, 16 - 2 * depth), (0, width - in_rows)))
    cuts = np.cumsum([count * mix_rows, n_in, out_parts * mix_rows, n_in]).tolist()
    value_sums = flat_sum(2)
    rows_list = [flat_sum(1)[:n_in], flat_sum(0), value_sums[:, :width], value_sums[:, width:]]
    outs = [flat_sum(1)[n_in:]]
    for layer in range(1, depth):
        mix, gate, out, side_a, side_b = jnp.split(held[layer], cuts, axis=0)
        outs.append(out)
        rows_list += [gate, mix, side_a, side_b]
    last, last_cuts = owner_pieces(rows_list + [norm_own.reshape(count * 16, width)])
    own_sum, last = together(own_sum, last)
    last = lax.all_to_all(last, "seq", 0, 0, tiled=True)
    ssm_sum, last = gather_bits(own_sum, "dp", dp, far_first(dp), last)
    ssm_sum = ssm_sum.astype(F32)
    back_parts = jnp.split(last, last_cuts, axis=1)
    norm_came = back_parts.pop()
    back = back_parts
    norm_sum = jnp.sum(norm_came[:, : 2 * depth, :in_rows].astype(F32), 0).reshape(depth, 2, in_rows)

    def columns(block):
        cut = block.reshape(count, -1, dp, share).transpose(1, 2, 0, 3)
        return cut.reshape(-1, gate_width).astype(F32)

    def value_share(sides):
        sides = jnp.stack(sides, 0)
        return sides.transpose(2, 0, 1, 3).reshape(in_rows, 2 * count * width).astype(F32)

    def out_share(block):
        return block.reshape(out_parts, mix_rows, width).transpose(1, 0, 2).reshape(mix_rows, model).astype(F32)

    gates, mixes, values = [], [], []
    for layer in range(depth):
        gate, mix, side_a, side_b = back[4 * layer : 4 * layer + 4]
        gates.append(columns(gate))
        mixes.append(columns(mix))
        values.append(value_share([side_a, side_b]))
    outs = [out_share(out) for out in outs]

    state_sum = ssm_sum[:, : 2 * depth * own].reshape(dp, depth, 2, own, both).transpose(1, 2, 0, 3, 4)
    coef_sum, rate_sum = state_sum[:, 0], state_sum[:, 1]
    skip_sum = ssm_sum[:, 2 * depth * own :].reshape(dp, 16, lanes)[:, :depth, : 2 * own].transpose(1, 0, 2)
    return (
        stream,
        grad_stream,
        jnp.stack(gates),
        jnp.stack(values),
        jnp.stack(mixes),
        jnp.stack(outs),
        norm_sum[:, 0],
        norm_sum[:, 1],
        coef_sum.reshape(ssm_coef.shape),
        rate_sum.reshape(ssm_rate.shape),
        skip_sum.reshape(ssm_skip.shape),
    )


def solution(mesh):
    in_specs = (
        P(("dp", "seq"), None),
        P("dp"),
        P(("dp", "seq"), None),
        P(None, ("dp", "seq"), None),
        P(None, ("dp", "seq"), None),
        P(None, ("dp", "seq"), None),
        P(None, ("dp", "seq"), None),
        P(None, ("dp", "seq")),
        P(None, ("dp", "seq")),
        P(None, None, "seq", None),
        P(None, None, "seq", None),
        P(None, None, "seq"),
    )
    out_specs = (
        P(("dp", "seq"), None),
        P(("dp", "seq"), None),
        P(None, ("dp", "seq"), None),
        P(None, ("dp", "seq"), None),
        P(None, ("dp", "seq"), None),
        P(None, ("dp", "seq"), None),
        P(None, ("dp", "seq")),
        P(None, ("dp", "seq")),
        P(None, None, "seq", None),
        P(None, None, "seq", None),
        P(None, None, "seq"),
    )
    return jax.shard_map(shards, mesh=mesh, in_specs=in_specs, out_specs=out_specs, check_vma=False)
```
